32 devices in a mesh: dp: 4 (over y, core), expert: 8 (over z, x).
Axes of the slice: x: 2, y: 2, z: 4, core: 2. Of those that a mesh axis runs over, the one named last changes fastest.
Arguments:
- queries: bfloat16 [4, 1024, 2048], P('dp', 'expert'), may hold values from -5.5 to 5.5
- keys: bfloat16 [4, 1024, 2048], P('dp', 'expert'), may hold values from -5.5 to 5.5
- values: bfloat16 [4, 1024, 2048], P('dp', 'expert'), may hold values from -6 to 6
- doc_ids: int32 [4, 1024], P('dp', 'expert'), may hold values from 0 to 3, never falling along the last dimension, each value on 1 to 512 neighbouring positions
- expert_index: int32 [4, 1024, 2], P('dp', 'expert'), may hold values from 0 to 7, all different within a row; in each aligned block of 128 rows (0 to 127, 128 to 255, ..., all dimensions but the last counted through in order) at most 48 rows name the same one
- gates: float32 [4, 1024, 2], P('dp', 'expert'), may hold values from 0.1 to 1
- capacity: int32 [8], replicated, may hold values from 24 to 48, as said below
- norm_gain: float32 [2048], replicated, may hold values from 0.1 to 1.9
- gate_weight: bfloat16 [8, 2048, 1024], P('expert', 'dp'), may hold values from -0.125 to 0.125
- up_weight: bfloat16 [8, 2048, 1024], P('expert', 'dp'), may hold values from -0.125 to 0.125
- down_weight: bfloat16 [8, 1024, 2048], P('expert', 'dp'), may hold values from -0.1875 to 0.1875
Outputs:
- mixed: bfloat16 [4, 1024, 2048], P('dp', 'expert')
The draws below stay inside these ranges and needn't reach their ends.
Inputs may be any that keep to these rules, and one draw needn't show every extreme that they name: `doc_ids`: never falls along a window; each protein has 1 to 512 residues, one exactly 512; every number of proteins below 4 appears. `expert_index`: the two experts of a residue differ; within the 128 residues of one device (aligned blocks of a window) no expert is named by more than 48 residues, a bound that some block reaches. Some expert has capacity exactly 48.
All inputs are finite; a program needn't handle non-finite values.
Results may differ from the reference program's by a relative error of at most 0.017.
Values may be sent and summed in bfloat16 or wider, within the bound.
No kernel may reach another device: no remote copies, remote signals or barrier semaphores. Data moves between devices by JAX's collectives and lax.ppermute only.
A program may use at most 64 MiB of HBM per device.

```python
import math
import jax
import jax.numpy as jnp
import numpy as np
from jax import lax

HEAD_DIM = 128
D = 2048
FF = 1024
TOP = 2
WINDOW = 512
TOK_DEV = 128
EXPERTS = 8
WINDOWS = 4
LENGTH = 1024
MOST = 48
DOCS = 4
DOC_MOST = 512


def base_field(key):
    return jnp.clip(jax.random.normal(key, (WINDOWS, LENGTH, D), jnp.float32), -4.0, 4.0)


def draw_queries(key, part):
    drawn = base_field(jax.random.fold_in(key, 31))
    return drawn.astype(jnp.bfloat16)


def draw_keys(key, part):
    drawn = base_field(jax.random.fold_in(key, 32))
    return drawn.astype(jnp.bfloat16)


def draw_capacity(key, part):
    limits = jax.random.randint(jax.random.fold_in(key, 21), (EXPERTS,), (MOST + 1) // 2, MOST + 1)
    fullest = jax.random.randint(jax.random.fold_in(key, 22), (), 0, EXPERTS)
    return jnp.where(jnp.arange(EXPERTS, dtype=jnp.int32) == fullest, MOST, limits).astype(jnp.int32)


def steps_of(rng, shape, pieces, smallest, top_value):
    gain = 1.0
    for axis_at, parts in pieces:
        draws = jax.random.uniform(jax.random.fold_in(jax.random.fold_in(rng, 6), axis_at), (parts,), jnp.float32, smallest / len(pieces), top_value / len(pieces))
        gain = gain * jnp.repeat(jnp.exp(draws), shape[axis_at] // parts).reshape((-1,) + (1,) * (len(shape) - 1 - axis_at))
    return gain


def length_profile(number_of, total, bound, slope):
    portions = [(1 << 20) // math.isqrt(standing ** slope) + 1 for standing in range(2, number_of + 1)]
    rest, given = total - bound - (number_of - 1), [1] * (number_of - 1)
    while rest > 0:
        candidates = [i for i in range(number_of - 1) if given[i] < bound]
        mass, remaining = sum([portions[i] for i in candidates]), rest
        for i in candidates:
            extra = min(bound - given[i], max(1, remaining * portions[i] // mass), rest)
            given[i] = given[i] + extra
            rest = rest - extra
    return np.array([bound] + given)


def uneven(key, number_of, total, limit, slope):
    if number_of == 2:
        one = jax.random.randint(key, (), max(1, total - limit), min(limit, total - 1) + 1)
        return jnp.stack([one, total - one])
    lengths = jnp.asarray(length_profile(number_of, total, limit, slope), jnp.int32)
    twos = (number_of - 1) // 2
    source_of, sink = lengths[1:1 + 2 * twos:2], lengths[2:2 + 2 * twos:2]
    slack = jnp.minimum(source_of - 1, limit - sink)
    moved = jax.random.randint(jax.random.fold_in(key, 1), (twos,), 0, 1 << 20) % (slack + 1)
    lengths = lengths.at[1:1 + 2 * twos:2].set(source_of - moved).at[2:2 + 2 * twos:2].set(sink + moved)
    return lengths[jax.random.permutation(jax.random.fold_in(key, 2), number_of)]


def routed_block(stream_key, own, number, rows, amount, top, bound, skew):
    order = jax.random.permutation(stream_key, amount)
    heavy_load, ordinary = shares(amount, rows * top, bound, skew, True), shares(amount, rows * top, bound, skew, False)
    places = jnp.arange(amount)

    def named(tallies, offset_by):
        used = int((tallies > 0).sum())
        fixed = max(1, used // 4)
        passed = fixed + (places - fixed + offset_by * (used - fixed)) % max(1, amount - fixed)
        return jnp.zeros((amount,), jnp.int32).at[order[jnp.where(places < fixed, places, passed)]].set(jnp.asarray(tallies, jnp.int32))

    tallies = jnp.where(number % 4 == 0, named(heavy_load, number // 4), named(ordinary, number - number // 4 - 1))
    mixed = jax.random.permutation(jax.random.fold_in(own, 3), amount)
    donor, sink = mixed[0:amount // 2 * 2:2], mixed[1:amount // 2 * 2:2]
    margin = jnp.minimum(tallies[donor] - 1, bound - tallies[sink]) // 2
    margin = jnp.where((donor == order[0]) | (sink == order[0]) | (tallies[sink] == 0), 0, jnp.maximum(margin, 0))
    passed = jax.random.randint(jax.random.fold_in(own, 4), (amount // 2,), 0, 1 << 20) % (margin + 1)
    tallies = tallies.at[donor].add(-passed).at[sink].add(passed)
    members = jnp.searchsorted(jnp.cumsum(tallies), jnp.arange(rows * top), side="right").astype(jnp.int32)
    table = members.reshape(top, rows).T
    table = table[jax.random.permutation(jax.random.fold_in(own, 1), rows)]
    offset_by = jax.random.randint(jax.random.fold_in(own, 2), (rows, 1), 0, top)
    return jnp.take_along_axis(table, (jnp.arange(top)[None, :] + offset_by) % top, axis=1)


def shares(count, total, limit, lean, full):
    portions = [(1 << 20) // math.isqrt(standing ** lean) + 1 for standing in range(1, count + 1)]
    largest = limit if full else min(limit, max(-(-total // count), total * portions[0] // sum(portions)))
    least = 1 if total - largest >= count - 1 else 0
    holding, rest = [largest] + [least] * (count - 1), total - largest - least * (count - 1)
    while rest > 0:
        movable = [i for i in range(1, count) if holding[i] < largest] or [i for i in range(1, count) if holding[i] < limit]
        pool, left = sum([portions[i] for i in movable]), rest
        for i in movable:
            extra = min(limit - holding[i], max(1, left * portions[i] // pool), rest)
            holding[i] = holding[i] + extra
            rest = rest - extra
    return np.array(holding)


def scatter_about(stream_key, dims, spread, bound, split=(), held_as=jnp.bfloat16):
    values = jax.random.normal(stream_key, dims, jnp.float32) * spread
    if len(split) > 0:
        values = steps_of(stream_key, dims, split, -0.22, 0.18) * values
    return jnp.clip(values, min=-bound, max=bound).astype(held_as)


def setup_inputs(seed: int = 0) -> dict:
    splits = jax.random.split(jax.random.key(seed), 12)
    queries = draw_queries(jax.random.fold_in(splits[11], 71), 0)
    keys = draw_keys(jax.random.fold_in(splits[11], 71), 0)
    values = scatter_about(splits[2], (WINDOWS, LENGTH, D), 1.0, 6.0, ((0, 4), (1, 8)))
    doc_ids = jax.vmap(lambda own: jnp.searchsorted(jnp.cumsum(uneven(own, DOCS, LENGTH, DOC_MOST, 1)), jnp.arange(LENGTH), side="right"))(jax.random.split(splits[3], WINDOWS)).reshape((WINDOWS, LENGTH)).astype(jnp.int32)
    expert_index_keys = jax.random.split(jax.random.fold_in(splits[4], 1), WINDOWS * LENGTH // TOK_DEV)
    expert_index_turns = jax.random.permutation(jax.random.fold_in(splits[4], 3), WINDOWS * LENGTH // TOK_DEV)
    expert_index = jax.vmap(lambda own, number: routed_block(jax.random.fold_in(splits[4], 2), own, number, TOK_DEV, EXPERTS, TOP, MOST, 2))(expert_index_keys, expert_index_turns).reshape((WINDOWS, LENGTH, TOP))
    gates = jnp.clip(jnp.exp(math.log(1.0) - 2.3025851 * jax.random.uniform(splits[5], (WINDOWS, LENGTH, TOP), jnp.float32) ** steps_of(splits[5], (WINDOWS, LENGTH, TOP), ((0, 4), (1, 8)), -0.2, 0.2)), 0.1, 1.0)
    capacity = draw_capacity(jax.random.fold_in(splits[11], 71), 0)
    norm_gain = jnp.clip(1.0 + 0.18 * jax.random.normal(splits[7], (D,), jnp.float32), 0.1, 1.9)
    gate_weight = scatter_about(splits[8], (EXPERTS, D, FF), D ** -0.5, 0.125, ((0, 8), (1, 4)))
    up_weight = scatter_about(splits[9], (EXPERTS, D, FF), D ** -0.5, 0.125, ((0, 8), (1, 4)))
    down_weight = scatter_about(splits[10], (EXPERTS, FF, D), FF ** -0.5, 0.1875, ((0, 8), (1, 4)))
    return dict(queries=queries, keys=keys, values=values, doc_ids=doc_ids, expert_index=expert_index, gates=gates, capacity=capacity, norm_gain=norm_gain, gate_weight=gate_weight, up_weight=up_weight, down_weight=down_weight)


def attend_window(queries, keys, values, doc_row):
    length = queries.shape[0]
    width = queries.shape[1]
    heads = width // HEAD_DIM
    q_block = min(512, length)
    keys_pad = jnp.pad(keys, ((WINDOW, 0), (0, 0)))
    values_pad = jnp.pad(values, ((WINDOW, 0), (0, 0)))
    docs_pad = jnp.pad(doc_row, (WINDOW, 0), constant_values=-1)

    def one_block(number):
        begin = number * q_block
        query_rows = lax.dynamic_slice_in_dim(queries, begin, q_block, 0).astype(jnp.float32).reshape(q_block, heads, HEAD_DIM)
        key_rows = lax.dynamic_slice_in_dim(keys_pad, begin, q_block + WINDOW, 0).astype(jnp.float32).reshape(q_block + WINDOW, heads, HEAD_DIM)
        value_rows = lax.dynamic_slice_in_dim(values_pad, begin, q_block + WINDOW, 0).astype(jnp.float32).reshape(q_block + WINDOW, heads, HEAD_DIM)
        query_docs = lax.dynamic_slice_in_dim(doc_row, begin, q_block, 0)
        key_docs = lax.dynamic_slice_in_dim(docs_pad, begin, q_block + WINDOW, 0)
        query_pos = begin + jnp.arange(q_block, dtype=jnp.int32)
        key_pos = begin - WINDOW + jnp.arange(q_block + WINDOW, dtype=jnp.int32)
        allowed = (key_pos[None, :] <= query_pos[:, None]) & (key_pos[None, :] > query_pos[:, None] - WINDOW) & (key_docs[None, :] == query_docs[:, None])
        scores = jnp.einsum('qhd,khd->hqk', query_rows, key_rows) * (1.0 / math.sqrt(HEAD_DIM))
        scores = jnp.where(allowed[None], scores, -1e+30)
        highest = lax.optimization_barrier(jnp.max(scores, axis=-1, keepdims=True))
        expo = jnp.exp(scores - highest)
        probs = (expo / lax.optimization_barrier(jnp.sum(expo, axis=-1, keepdims=True))).astype(jnp.bfloat16)
        result = jnp.einsum('hqk,khd->qhd', probs.astype(jnp.float32), value_rows)
        return result.reshape(q_block, width).astype(jnp.bfloat16)
    blocks = lax.map(one_block, jnp.arange(length // q_block, dtype=jnp.int32))
    return blocks.reshape(length, width)

def expert_block(rows, w_gate, w_up, w_down):
    gate = jnp.dot(rows, w_gate, preferred_element_type=jnp.float32)
    upward = jnp.dot(rows, w_up, preferred_element_type=jnp.float32)
    hidden = (jax.nn.silu(gate) * upward).astype(jnp.bfloat16)
    return jnp.dot(hidden, w_down, preferred_element_type=jnp.float32).astype(jnp.bfloat16)

def reference(queries, keys, values, doc_ids, expert_index, gates, capacity, norm_gain, gate_weight, up_weight, down_weight):
    attended = lax.map(lambda packed: attend_window(packed[0], packed[1], packed[2], packed[3]), (queries, keys, values, doc_ids))
    flat_att = attended.reshape(-1, D).astype(jnp.float32)
    normed = (flat_att * lax.rsqrt(lax.optimization_barrier(jnp.mean(flat_att * flat_att, axis=-1, keepdims=True)) + 1e-05) * norm_gain).astype(jnp.bfloat16)
    total_rows = flat_att.shape[0]
    blocks = total_rows // TOK_DEV
    chosen = expert_index.reshape(blocks, TOK_DEV * TOP)
    onehot = (chosen[..., None] == jnp.arange(EXPERTS, dtype=jnp.int32)).astype(jnp.int32)
    ranks = lax.optimization_barrier(jnp.sum(onehot * (jnp.cumsum(onehot, axis=1) - 1), axis=-1))
    limits = lax.optimization_barrier(jnp.sum(onehot * capacity, axis=-1))
    kept_flat = (ranks < limits).reshape(-1)
    chosen_flat = chosen.reshape(-1)
    ranks_flat = ranks.reshape(-1)
    assign_ids = jnp.arange(total_rows * TOP, dtype=jnp.int32)
    block_id = assign_ids // (TOK_DEV * TOP)
    slot = block_id * MOST + ranks_flat
    token = assign_ids // TOP
    span = blocks * MOST

    def run_expert(number):
        target = jnp.where((chosen_flat == number) & kept_flat, slot, span)
        slot_token = jnp.full((span,), -1, jnp.int32).at[target].set(token, mode='drop')
        rows = jnp.where((slot_token >= 0)[:, None], normed[jnp.maximum(slot_token, 0)], jnp.zeros((), jnp.bfloat16))
        return expert_block(rows, gate_weight[number], up_weight[number], down_weight[number])
    outputs = lax.map(run_expert, jnp.arange(EXPERTS, dtype=jnp.int32)).reshape(EXPERTS * span, D)
    where_from = jnp.where(kept_flat, chosen_flat * span + slot, 0)
    weight = jnp.where(kept_flat, gates.reshape(-1), 0.0).reshape(total_rows, TOP)
    picked = outputs[where_from].reshape(total_rows, TOP, D)
    combined = flat_att
    for which in range(TOP):
        combined = combined + picked[:, which].astype(jnp.float32) * weight[:, which:which + 1]
    return combined.astype(jnp.bfloat16).reshape(WINDOWS, LENGTH, D)
```

```python
import functools
import math

import jax
import jax.numpy as jnp
from jax import lax
from jax.experimental import pallas as pl
from jax.experimental.pallas import tpu as pltpu
from jax.sharding import PartitionSpec as P

HEAD_DIM = 128
TOP = 2
WINDOW = 512
META = 16
LANES = 128
F32 = jnp.float32
BF16 = jnp.bfloat16


def shifted_2(block, axis, distance):
    devices = range(lax.axis_size(axis))
    route = [(i - distance, i) for i in devices if i - distance in devices]
    return lax.ppermute(block, axis, route)


def attend_local(queries, key_rows, value_rows, query_docs, key_docs, query_start, key_start):
    rows_dev, width = queries.shape
    heads = width // HEAD_DIM
    q_block = min(512, rows_dev)
    before = key_rows.shape[0] - rows_dev

    def one_block(number):
        begin = number * q_block
        query_part = queries.reshape(q_block, heads, HEAD_DIM)
        key_part = key_rows.reshape(before + q_block, heads, HEAD_DIM)
        value_part = value_rows.reshape(before + q_block, heads, HEAD_DIM)
        query_pos = query_start + begin + jnp.arange(q_block, dtype=jnp.int32)
        key_pos = key_start + begin + jnp.arange(before + q_block, dtype=jnp.int32)
        allowed = (key_pos[None, :] <= query_pos[:, None]) & (
            key_pos[None, :] > query_pos[:, None] - WINDOW
        )
        allowed = allowed & (key_pos[None, :] >= 0) & (key_docs[None, :] == query_docs[:, None])
        scores = jnp.einsum(
            "qhd,khd->hqk", query_part, key_part, preferred_element_type=jnp.float32
        ) * (1.0 / math.sqrt(HEAD_DIM))
        scores = jnp.where(allowed[None], scores, -1e30)
        highest = jnp.max(scores, axis=-1, keepdims=True)
        expo = jnp.exp(scores - highest)
        probs = (expo / jnp.sum(expo, axis=-1, keepdims=True)).astype(jnp.bfloat16)
        result = jnp.einsum("hqk,khd->qhd", probs, value_part, preferred_element_type=jnp.float32)
        return result.reshape(q_block, width).astype(jnp.bfloat16)

    blocks = lax.map(one_block, jnp.arange(rows_dev // q_block, dtype=jnp.int32))
    return blocks.reshape(rows_dev, width)


def per_device_general(
    queries,
    keys,
    values,
    doc_ids,
    expert_index,
    gates,
    capacity,
    norm_gain,
    gate_weight,
    up_weight,
    down_weight,
):
    rows_dev = queries.shape[1]
    width = queries.shape[2]
    reach_back = (WINDOW - 1) // rows_dev + 1
    own_pair = jnp.stack([keys[0], values[0]], axis=0)
    own_docs = doc_ids[0].astype(jnp.bfloat16)
    earlier = []
    current = (own_pair, own_docs)
    for number in range(reach_back):
        current = shifted_2((current[0], current[1]), "expert", 1)
        earlier.insert(0, current)
    pair_all = jnp.concatenate([shifted[0] for shifted in earlier] + [own_pair], axis=1)
    docs_all = jnp.concatenate([shifted[1] for shifted in earlier] + [own_docs], axis=0)
    position = lax.axis_index("expert")
    attended = attend_local(
        queries[0],
        pair_all[0],
        pair_all[1],
        own_docs,
        docs_all,
        position * rows_dev,
        (position - reach_back) * rows_dev,
    )
    flat_att = attended.astype(jnp.float32)
    normed = (
        flat_att
        * lax.rsqrt(jnp.mean(flat_att * flat_att, axis=-1, keepdims=True) + 1e-05)
        * norm_gain
    ).astype(jnp.bfloat16)
    experts = lax.axis_size("expert")
    most = max(2, 3 * rows_dev * TOP // (2 * experts))
    chosen_flat = expert_index[0].reshape(-1)
    onehot = (chosen_flat[:, None] == jnp.arange(experts, dtype=jnp.int32)[None, :]).astype(
        jnp.int32
    )
    ranks = jnp.sum(onehot * (jnp.cumsum(onehot, axis=0) - 1), axis=1)
    limits = jnp.sum(onehot * capacity[None, :], axis=1)
    kept = ranks < limits
    slot = jnp.where(kept, chosen_flat * most + ranks, experts * most)
    token_of = jnp.arange(rows_dev * TOP, dtype=jnp.int32) // TOP
    slot_token = jnp.full((experts * most,), -1, jnp.int32).at[slot].set(token_of, mode="drop")
    filled = slot_token >= 0
    outgoing = jnp.where(
        filled[:, None], normed[jnp.maximum(slot_token, 0)], jnp.zeros((), jnp.bfloat16)
    )
    outgoing = outgoing.reshape(experts, most, width)
    received = lax.all_to_all(outgoing, "expert", split_axis=0, concat_axis=0, tiled=True)
    sources = received.shape[0]
    flat_rows = received.reshape(sources * most, width)
    columns = flat_rows
    gate_sum = jnp.dot(
        columns,
        lax.all_gather(gate_weight, "dp", axis=1, tiled=True)[0],
        preferred_element_type=jnp.float32,
    )
    up_sum = jnp.dot(
        columns,
        lax.all_gather(up_weight, "dp", axis=1, tiled=True)[0],
        preferred_element_type=jnp.float32,
    )
    hidden = (jax.nn.silu(gate_sum) * up_sum).astype(jnp.bfloat16)
    columns = hidden
    result = jnp.dot(
        columns,
        lax.all_gather(down_weight, "dp", axis=1, tiled=True)[0],
        preferred_element_type=jnp.float32,
    )
    answered = result.astype(jnp.bfloat16).reshape(sources, most, width)
    returned = lax.all_to_all(answered, "expert", split_axis=0, concat_axis=0, tiled=True)
    back_flat = returned.reshape(experts * most, width)
    picked = back_flat[jnp.minimum(slot, experts * most - 1)].reshape(rows_dev, TOP, width)
    weight = jnp.where(kept, gates[0].reshape(-1), 0.0).reshape(rows_dev, TOP)
    combined = flat_att
    for which in range(TOP):
        combined = combined + picked[:, which].astype(jnp.float32) * weight[:, which : which + 1]
    return combined.astype(jnp.bfloat16)[None]


def pack_kernel(*refs):
    out_ref, slots_ref = refs[7:9]
    copies = [pltpu.make_async_copy(refs[i], refs[9 + i], refs[16].at[i]) for i in range(7)]
    for number in (3, 4, 5, 6, 0, 1, 2):
        copies[number].start()
    q_ref, k_ref, v_ref, docs_ref, index_ref, gates_ref, limits_ref = refs[9:16]
    rows = q_ref.shape[1]
    owners, _, part = out_ref.shape
    experts = limits_ref.shape[1]
    most = most_of(rows, experts)
    for number in (3, 4, 5, 6):
        copies[number].wait()
    line = lax.broadcasted_iota(jnp.int32, (META, rows), 0)
    given = jnp.zeros((META, rows), F32)
    for k in range(TOP):
        given = jnp.where(line == k, index_ref[k : k + 1].astype(F32), given)
        given = jnp.where(line == TOP + k, gates_ref[k : k + 1], given)
    given = jnp.concatenate([given, jnp.zeros((rows - META, rows), F32)], axis=0).T
    index = [given[:, k : k + 1] for k in range(TOP)]
    names = lax.broadcasted_iota(jnp.int32, (rows, experts), 1).astype(F32)
    chosen = [jnp.where(index[k] == names, 1.0, 0.0) for k in range(TOP)]
    below = lax.broadcasted_iota(jnp.int32, (rows, rows), 1) < lax.broadcasted_iota(jnp.int32, (rows, rows), 0)
    earlier = jnp.dot(
        jnp.where(below, 1.0, 0.0).astype(BF16), (chosen[0] + chosen[1]).astype(BF16), preferred_element_type=F32
    )
    limits = limits_ref[...].astype(F32)
    columns = []
    slots = []
    weights = []
    for k in range(TOP):
        rank = jnp.sum(chosen[k] * earlier, axis=1, keepdims=True)
        limit = jnp.sum(chosen[k] * limits, axis=1, keepdims=True)
        slots.append(index[k] * most + rank)
        columns += [index[k], rank]
        weights.append(jnp.where(rank < limit, given[:, TOP + k : TOP + k + 1], 0.0))
    for weight in weights:
        first = weight.astype(BF16).astype(F32)
        second = (weight - first).astype(BF16).astype(F32)
        columns += [first, second, weight - first - second]
    lane = lax.broadcasted_iota(jnp.int32, (rows, LANES), 1)
    table = jnp.zeros((rows, LANES), F32)
    for number, column in enumerate(columns):
        table = jnp.where(lane == number + 1, column, table)
    turned = table.T[:META]
    turned = jnp.where(line == 0, docs_ref[...].astype(F32), turned).astype(BF16)
    slots_ref[...] = jnp.where(lane == 0, slots[0], jnp.where(lane == 1, slots[1], -1.0))
    for owner in range(owners):
        out_ref[owner, TOP_ROWS * rows :, :rows] = turned
        out_ref[owner, TOP_ROWS * rows :, rows:] = jnp.zeros((META, part - rows), BF16)
    for which, ref in enumerate((q_ref, k_ref, v_ref)):
        copies[which].wait()
        for owner in range(owners):
            out_ref[owner, which * rows : (which + 1) * rows, :] = ref[0, :, owner * part : (owner + 1) * part]


TOP_ROWS = 3


def most_of(rows, experts):
    return max(2, 3 * rows * TOP // (2 * experts))


def pack(queries, keys, values, doc_ids, expert_index, gates, capacity, owners):
    rows, width = queries.shape[1:]
    part = width // owners
    vmem = pl.BlockSpec(memory_space=pltpu.VMEM)
    given = (queries, keys, values, doc_ids, expert_index[0].T, gates[0].T, capacity[None, :])
    return pl.pallas_call(
        pack_kernel,
        out_shape=(
            jax.ShapeDtypeStruct((owners, TOP_ROWS * rows + META, part), BF16),
            jax.ShapeDtypeStruct((rows, LANES), F32),
        ),
        in_specs=[pl.BlockSpec(memory_space=pltpu.HBM)] * 7,
        out_specs=(vmem, vmem),
        scratch_shapes=[pltpu.VMEM(array.shape, array.dtype) for array in given] + [pltpu.SemaphoreType.DMA((7,))],
        compiler_params=pltpu.CompilerParams(vmem_limit_bytes=60 * 1024 * 1024),
        name="pack_by_heads",
    )(*given)


def attend_kernel(most, all_ref, out_ref):
    blocks, _, part = all_ref.shape
    rows = (all_ref.shape[1] - META) // TOP_ROWS
    experts = out_ref.shape[0]
    heads = part // HEAD_DIM
    reach = (WINDOW - 1) // rows + 1
    factor = math.log2(math.e) / math.sqrt(HEAD_DIM)
    apart = lax.broadcasted_iota(jnp.int32, (rows, rows), 0) - lax.broadcasted_iota(jnp.int32, (rows, rows), 1)
    slot_of = lax.broadcasted_iota(jnp.int32, (experts * most, rows), 0).astype(F32)

    @pl.loop(0, blocks)
    def _(number):
        meta = all_ref[number, TOP_ROWS * rows :, :rows].astype(F32)
        padded = jnp.concatenate([meta, jnp.zeros((rows - META, rows), F32)], axis=0)
        query_docs = padded.T[:, 0:1]
        sources = []
        allowed = []
        for step in range(reach + 1):
            source = number - reach + step
            held = jnp.maximum(source, 0)
            docs = all_ref[held, TOP_ROWS * rows :, :rows].astype(F32)[0:1]
            docs = jnp.where(source >= 0, docs, -1.0)
            mask = query_docs == docs
            offset = (reach - step) * rows
            if offset - (rows - 1) < 0:
                mask = mask & (apart + offset >= 0)
            if offset + (rows - 1) >= WINDOW:
                mask = mask & (apart + offset < WINDOW)
            sources.append(held)
            allowed.append(mask)
        done = []
        for head in range(heads):
            lanes = slice(head * HEAD_DIM, (head + 1) * HEAD_DIM)
            query = all_ref[number, 0:rows, lanes]
            scores = []
            for held, mask in zip(sources, allowed):
                key = all_ref[held, rows : 2 * rows, lanes]
                score = lax.dot_general(query, key, (((1,), (1,)), ((), ())), preferred_element_type=F32)
                scores.append(jnp.where(mask, score, -1e30))
            highest = functools.reduce(jnp.maximum, scores)
            highest = jnp.max(highest, axis=1, keepdims=True)
            expo = [jnp.exp2((score - highest) * factor) for score in scores]
            total = jnp.sum(functools.reduce(jnp.add, expo), axis=1, keepdims=True)
            result = jnp.zeros((rows, HEAD_DIM), F32)
            for held, weight in zip(sources, expo):
                value = all_ref[held, 2 * rows : 3 * rows, lanes]
                result = result + jnp.dot(weight.astype(BF16), value, preferred_element_type=F32)
            done.append((result / total).astype(BF16))
        attended = jnp.concatenate(done, axis=1)
        slots = [meta[1 + 2 * k : 2 + 2 * k] * most + meta[2 + 2 * k : 3 + 2 * k] for k in range(TOP)]
        picks = (slot_of == slots[0]) | (slot_of == slots[1])
        routed = jnp.dot(jnp.where(picks, 1.0, 0.0).astype(BF16), attended, preferred_element_type=F32).astype(BF16)
        for expert in range(experts):
            out_ref[expert, number] = routed[expert * most : (expert + 1) * most]


def attend(gathered, experts, most):
    blocks, _, part = gathered.shape
    vmem = pl.BlockSpec(memory_space=pltpu.VMEM)
    return pl.pallas_call(
        functools.partial(attend_kernel, most),
        out_shape=jax.ShapeDtypeStruct((experts, blocks, most, part), BF16),
        in_specs=[vmem],
        out_specs=vmem,
        compiler_params=pltpu.CompilerParams(vmem_limit_bytes=32 * 1024 * 1024),
        name="attend_and_route",
    )(gathered)


def expert_kernel(
    pieces, most, place_ref, rows_ref, meta_ref, gain_ref, *refs
):
    gate_refs, up_refs, down_refs = refs[:pieces], refs[pieces : 2 * pieces], refs[2 * pieces : 3 * pieces]
    out_ref, gate_all, up_all, down_all, normed, hidden, sems = refs[3 * pieces :]
    parts, count, part = rows_ref.shape
    blocks = meta_ref.shape[0]
    deep, wide = gate_all.shape[2], gate_all.shape[3]
    width = parts * part
    mine, expert = place_ref[0], place_ref[1]

    def gate_copies(step):
        tile = pl.ds(pl.multiple_of((mine ^ step) * wide, wide), wide)
        found = []
        for piece in range(pieces):
            found.append(
                pltpu.make_async_copy(gate_refs[piece].at[0, :, tile], gate_all.at[step, piece], sems.at[0, step, piece])
            )
            found.append(
                pltpu.make_async_copy(up_refs[piece].at[0, :, tile], up_all.at[step, piece], sems.at[1, step, piece])
            )
        return found

    def down_copy(piece):
        return pltpu.make_async_copy(down_refs[piece].at[0], down_all.at[piece], sems.at[2, 0, piece])

    for step in range(pieces):
        for copy in gate_copies(step):
            copy.start()
    for piece in range(pieces):
        down_copy(piece).start()

    squares = jnp.zeros((count, part), F32)
    for number in range(parts):
        held = rows_ref[number].astype(F32)
        squares = squares + held * held
    inverse = lax.rsqrt(jnp.sum(squares, axis=1, keepdims=True) / width + 1e-05)
    per_piece = deep // part
    for number in range(parts):
        held = rows_ref[number].astype(F32) * inverse * gain_ref[:, number * part : (number + 1) * part]
        place = number % per_piece
        normed[number // per_piece, :, place * part : (place + 1) * part] = held.astype(BF16)

    @pl.loop(0, pieces)
    def _(step):
        for copy in gate_copies(step):
            copy.wait()
        gate = jnp.zeros((count, wide), F32)
        up = jnp.zeros((count, wide), F32)
        for piece in range(pieces):
            held = normed[mine ^ piece]
            gate = gate + jnp.dot(held, gate_all[step, piece], preferred_element_type=F32)
            up = up + jnp.dot(held, up_all[step, piece], preferred_element_type=F32)
        hidden[step] = (gate / (1.0 + jnp.exp(-gate)) * up).astype(BF16)

    for piece in range(pieces):
        down_copy(piece).wait()

    rows = meta_ref.shape[2] if meta_ref.shape[2] < LANES else LANES
    slot_of = lax.broadcasted_iota(jnp.int32, (most, rows), 0).astype(F32) + (expert * most).astype(F32)
    weights, firsts = [], []
    for number in range(blocks):
        meta = meta_ref[number, :, :rows].astype(F32)
        total = jnp.zeros((most, rows), F32)
        for k in range(TOP):
            slot = meta[1 + 2 * k : 2 + 2 * k] * most + meta[2 + 2 * k : 3 + 2 * k]
            at = 1 + 2 * TOP + 3 * k
            weight = meta[at : at + 1] + meta[at + 1 : at + 2] + meta[at + 2 : at + 3]
            total = total + jnp.where(slot_of == slot, weight, 0.0)
            if k == 0:
                firsts.append(jnp.sum(jnp.where(slot_of == slot, 1.0, 0.0), axis=1, keepdims=True))
        weights.append(jnp.sum(total, axis=1, keepdims=True))
    weight = jnp.concatenate(weights, axis=0)
    first = jnp.concatenate(firsts, axis=0)

    for number in range(parts):
        lanes = slice(number * part, (number + 1) * part)
        result = jnp.zeros((count, part), F32)
        for piece in range(pieces):
            result = result + jnp.dot(hidden[piece], down_all[piece, :, lanes], preferred_element_type=F32)
        result = result.astype(BF16).astype(F32) * weight
        out_ref[:, lanes] = (rows_ref[number].astype(F32) * first + result).astype(BF16)


def run_expert(rows, gathered, gain, gates, ups, downs, most):
    parts, count, part = rows.shape
    pieces = len(gates)
    width = parts * part
    _, deep, hidden = gates[0].shape
    wide = hidden // pieces
    blocks, deepest, _ = gathered.shape
    place = jnp.stack([lax.axis_index("dp"), lax.axis_index("expert")]).astype(jnp.int32)
    vmem = pl.BlockSpec(memory_space=pltpu.VMEM)
    anywhere = pl.BlockSpec(memory_space=pltpu.HBM)
    meta_at = deepest // META - 1
    grid = pltpu.PrefetchScalarGridSpec(
        num_scalar_prefetch=1,
        grid=(1,),
        in_specs=[
            pl.BlockSpec((parts, count, part), lambda i, _: (0, 0, 0)),
            pl.BlockSpec((blocks, META, part), lambda i, _: (0, meta_at, 0)),
            pl.BlockSpec((1, width), lambda i, _: (0, 0)),
        ]
        + [anywhere] * (3 * pieces),
        out_specs=pl.BlockSpec((count, width), lambda i, _: (0, 0)),
        scratch_shapes=[
            pltpu.VMEM((pieces, pieces, deep, wide), BF16),
            pltpu.VMEM((pieces, pieces, deep, wide), BF16),
            pltpu.VMEM((pieces, wide, width), BF16),
            pltpu.VMEM((pieces, count, deep), BF16),
            pltpu.VMEM((pieces, count, wide), BF16),
            pltpu.SemaphoreType.DMA((3, pieces, pieces)),
        ],
    )
    return pl.pallas_call(
        functools.partial(expert_kernel, pieces, most),
        out_shape=jax.ShapeDtypeStruct((count, width), BF16),
        grid_spec=grid,
        compiler_params=pltpu.CompilerParams(vmem_limit_bytes=60 * 1024 * 1024),
        name="expert_rows",
    )(place, rows, gathered, gain[None, :], *gates, *ups, *downs)


def combine_kernel(rows_ref, slots_ref, out_ref):
    count = rows_ref.shape[0]
    rows = slots_ref.shape[0]
    slot_of = lax.broadcasted_iota(jnp.int32, (rows, count), 1).astype(F32)
    picks = (slot_of == slots_ref[:, 0:1]) | (slot_of == slots_ref[:, 1:2])
    picks = jnp.where(picks, 1.0, 0.0).astype(BF16)
    out_ref[0] = jnp.dot(picks, rows_ref[...], preferred_element_type=F32).astype(BF16)


def combine(returned, slots):
    vmem = pl.BlockSpec(memory_space=pltpu.VMEM)
    return pl.pallas_call(
        combine_kernel,
        out_shape=jax.ShapeDtypeStruct((1, slots.shape[0], returned.shape[1]), BF16),
        in_specs=[vmem] * 2,
        out_specs=vmem,
        compiler_params=pltpu.CompilerParams(vmem_limit_bytes=32 * 1024 * 1024),
        name="combine_choices",
    )(returned, slots)


def flipped(block, axis, bits):
    return lax.ppermute(block, axis, [(i, i ^ bits) for i in range(lax.axis_size(axis))])


def spread_weight(block, far):
    size = lax.axis_size("dp")
    bits = size // 2
    pieces = {0: block, bits: far}
    while bits > 1:
        bits //= 2
        for number in sorted(pieces):
            pieces[number | bits] = flipped(pieces[number], "dp", bits)
    return [pieces[number] for number in range(size)]


def per_device(
    queries,
    keys,
    values,
    doc_ids,
    expert_index,
    gates,
    capacity,
    norm_gain,
    gate_weight,
    up_weight,
    down_weight,
):
    rows, width = queries.shape[1:]
    experts = lax.axis_size("expert")
    most = most_of(rows, experts)
    over = lax.axis_size("dp")
    gate_far = flipped(gate_weight, "dp", over // 2)
    up_far = flipped(up_weight, "dp", over // 2)
    packed, slots = pack(queries, keys, values, doc_ids, expert_index, gates, capacity, experts)
    gathered = lax.all_to_all(packed, "expert", 0, 0, tiled=True)
    gathered, gate_far, up_far = lax.optimization_barrier((gathered, gate_far, up_far))
    gate_pieces = spread_weight(gate_weight, gate_far)
    up_pieces = spread_weight(up_weight, up_far)
    down_pieces = spread_weight(down_weight, flipped(down_weight, "dp", over // 2))
    routed = attend(gathered, experts, most)
    received = lax.all_to_all(routed, "expert", 0, 0, tiled=True)
    received = received.reshape(experts, experts * most, width // experts)
    answered = run_expert(received, gathered, norm_gain, gate_pieces, up_pieces, down_pieces, most)
    answered = answered.reshape(experts, most, width)
    returned = lax.all_to_all(answered, "expert", 0, 0, tiled=True)
    return combine(returned.reshape(experts * most, width), slots)


def by_heads(mesh, queries, gate_weight):
    over, experts = mesh.shape["dp"], mesh.shape["expert"]
    rows, width = queries.shape[1] // experts, queries.shape[2]
    hidden = gate_weight.shape[2]
    return (
        width % (experts * HEAD_DIM) == 0
        and rows == LANES
        and width // experts > rows
        and (width // over) % (width // experts) == 0
        and hidden % (over * LANES) == 0
        and most_of(rows, experts) % 16 == 0
        and over & (over - 1) == 0
        and queries.shape[0] == over
        and gate_weight.shape[0] == experts
    )


def solution(mesh):
    placed = (
        P("dp", "expert", None),
        P("dp", "expert", None),
        P("dp", "expert", None),
        P("dp", "expert"),
        P("dp", "expert", None),
        P("dp", "expert", None),
        P(),
        P(),
        P("expert", "dp", None),
        P("expert", "dp", None),
        P("expert", "dp", None),
    )

    def layer(*arrays):
        step = per_device if by_heads(mesh, arrays[0], arrays[8]) else per_device_general
        return jax.shard_map(
            step, mesh=mesh, in_specs=placed, out_specs=P("dp", "expert", None), check_vma=False
        )(*arrays)

    return layer
```

```python
import functools
import math

import jax
import jax.numpy as jnp
from jax import lax
from jax.experimental import pallas as pl
from jax.experimental.pallas import tpu as pltpu
from jax.sharding import PartitionSpec as P

HEAD_DIM = 128
TOP = 2
WINDOW = 512
META = 16
LANES = 128
F32 = jnp.float32
BF16 = jnp.bfloat16


def shifted_2(block, axis, distance):
    devices = range(lax.axis_size(axis))
    route = [(i - distance, i) for i in devices if i - distance in devices]
    return lax.ppermute(block, axis, route)


def attend_local(queries, key_rows, value_rows, query_docs, key_docs, query_start, key_start):
    rows_dev, width = queries.shape
    heads = width // HEAD_DIM
    q_block = min(512, rows_dev)
    before = key_rows.shape[0] - rows_dev

    def one_block(number):
        begin = number * q_block
        query_part = queries.reshape(q_block, heads, HEAD_DIM)
        key_part = key_rows.reshape(before + q_block, heads, HEAD_DIM)
        value_part = value_rows.reshape(before + q_block, heads, HEAD_DIM)
        query_pos = query_start + begin + jnp.arange(q_block, dtype=jnp.int32)
        key_pos = key_start + begin + jnp.arange(before + q_block, dtype=jnp.int32)
        allowed = (key_pos[None, :] <= query_pos[:, None]) & (
            key_pos[None, :] > query_pos[:, None] - WINDOW
        )
        allowed = allowed & (key_pos[None, :] >= 0) & (key_docs[None, :] == query_docs[:, None])
        scores = jnp.einsum(
            "qhd,khd->hqk", query_part, key_part, preferred_element_type=jnp.float32
        ) * (1.0 / math.sqrt(HEAD_DIM))
        scores = jnp.where(allowed[None], scores, -1e30)
        highest = jnp.max(scores, axis=-1, keepdims=True)
        expo = jnp.exp(scores - highest)
        probs = (expo / jnp.sum(expo, axis=-1, keepdims=True)).astype(jnp.bfloat16)
        result = jnp.einsum("hqk,khd->qhd", probs, value_part, preferred_element_type=jnp.float32)
        return result.reshape(q_block, width).astype(jnp.bfloat16)

    blocks = lax.map(one_block, jnp.arange(rows_dev // q_block, dtype=jnp.int32))
    return blocks.reshape(rows_dev, width)


def per_device_general(
    queries,
    keys,
    values,
    doc_ids,
    expert_index,
    gates,
    capacity,
    norm_gain,
    gate_weight,
    up_weight,
    down_weight,
):
    rows_dev = queries.shape[1]
    width = queries.shape[2]
    reach_back = (WINDOW - 1) // rows_dev + 1
    own_pair = jnp.stack([keys[0], values[0]], axis=0)
    own_docs = doc_ids[0].astype(jnp.bfloat16)
    earlier = []
    current = (own_pair, own_docs)
    for number in range(reach_back):
        current = shifted_2((current[0], current[1]), "expert", 1)
        earlier.insert(0, current)
    pair_all = jnp.concatenate([shifted[0] for shifted in earlier] + [own_pair], axis=1)
    docs_all = jnp.concatenate([shifted[1] for shifted in earlier] + [own_docs], axis=0)
    position = lax.axis_index("expert")
    attended = attend_local(
        queries[0],
        pair_all[0],
        pair_all[1],
        own_docs,
        docs_all,
        position * rows_dev,
        (position - reach_back) * rows_dev,
    )
    flat_att = attended.astype(jnp.float32)
    normed = (
        flat_att
        * lax.rsqrt(jnp.mean(flat_att * flat_att, axis=-1, keepdims=True) + 1e-05)
        * norm_gain
    ).astype(jnp.bfloat16)
    experts = lax.axis_size("expert")
    most = max(2, 3 * rows_dev * TOP // (2 * experts))
    chosen_flat = expert_index[0].reshape(-1)
    onehot = (chosen_flat[:, None] == jnp.arange(experts, dtype=jnp.int32)[None, :]).astype(
        jnp.int32
    )
    ranks = jnp.sum(onehot * (jnp.cumsum(onehot, axis=0) - 1), axis=1)
    limits = jnp.sum(onehot * capacity[None, :], axis=1)
    kept = ranks < limits
    slot = jnp.where(kept, chosen_flat * most + ranks, experts * most)
    token_of = jnp.arange(rows_dev * TOP, dtype=jnp.int32) // TOP
    slot_token = jnp.full((experts * most,), -1, jnp.int32).at[slot].set(token_of, mode="drop")
    filled = slot_token >= 0
    outgoing = jnp.where(
        filled[:, None], normed[jnp.maximum(slot_token, 0)], jnp.zeros((), jnp.bfloat16)
    )
    outgoing = outgoing.reshape(experts, most, width)
    received = lax.all_to_all(outgoing, "expert", split_axis=0, concat_axis=0, tiled=True)
    sources = received.shape[0]
    flat_rows = received.reshape(sources * most, width)
    columns = flat_rows
    gate_sum = jnp.dot(
        columns,
        lax.all_gather(gate_weight, "dp", axis=1, tiled=True)[0],
        preferred_element_type=jnp.float32,
    )
    up_sum = jnp.dot(
        columns,
        lax.all_gather(up_weight, "dp", axis=1, tiled=True)[0],
        preferred_element_type=jnp.float32,
    )
    hidden = (jax.nn.silu(gate_sum) * up_sum).astype(jnp.bfloat16)
    columns = hidden
    result = jnp.dot(
        columns,
        lax.all_gather(down_weight, "dp", axis=1, tiled=True)[0],
        preferred_element_type=jnp.float32,
    )
    answered = result.astype(jnp.bfloat16).reshape(sources, most, width)
    returned = lax.all_to_all(answered, "expert", split_axis=0, concat_axis=0, tiled=True)
    back_flat = returned.reshape(experts * most, width)
    picked = back_flat[jnp.minimum(slot, experts * most - 1)].reshape(rows_dev, TOP, width)
    weight = jnp.where(kept, gates[0].reshape(-1), 0.0).reshape(rows_dev, TOP)
    combined = flat_att
    for which in range(TOP):
        combined = combined + picked[:, which].astype(jnp.float32) * weight[:, which : which + 1]
    return combined.astype(jnp.bfloat16)[None]


def pack_kernel(owners, q_ref, k_ref, v_ref, *refs):
    given, out_refs, slots_ref = refs[:4], refs[4 : 4 + owners], refs[4 + owners]
    small, packed, sems, small_sems, store_sems = refs[5 + owners : 9 + owners], *refs[9 + owners :]
    rows = q_ref.shape[1]
    part = packed.shape[2]
    me = lax.axis_index("expert")
    order = list(range(owners // 2, owners)) + list(range(owners // 2))
    fetches = [pltpu.make_async_copy(given[i], small[i], small_sems.at[i]) for i in range(4)]
    for fetch in fetches:
        fetch.start()
    loads = {}
    for turn in order:
        lanes = pl.ds(pl.multiple_of((me ^ turn) * part, part), part)
        for which, ref in enumerate((q_ref, k_ref, v_ref)):
            loads[turn, which] = pltpu.make_async_copy(
                ref.at[0, :, lanes], packed.at[turn, pl.ds(which * rows, rows)], sems.at[turn, which]
            )
            loads[turn, which].start()
    for fetch in fetches:
        fetch.wait()
    docs_ref, index_ref, gates_ref, limits_ref = small
    experts = limits_ref.shape[1]
    most = most_of(rows, experts)
    line = lax.broadcasted_iota(jnp.int32, (META, rows), 0)
    given = jnp.zeros((META, rows), F32)
    for k in range(TOP):
        given = jnp.where(line == k, index_ref[k : k + 1].astype(F32), given)
        given = jnp.where(line == TOP + k, gates_ref[k : k + 1], given)
    given = jnp.concatenate([given, jnp.zeros((rows - META, rows), F32)], axis=0).T
    index = [given[:, k : k + 1] for k in range(TOP)]
    names = lax.broadcasted_iota(jnp.int32, (rows, experts), 1).astype(F32)
    chosen = [jnp.where(index[k] == names, 1.0, 0.0) for k in range(TOP)]
    below = lax.broadcasted_iota(jnp.int32, (rows, rows), 1) < lax.broadcasted_iota(jnp.int32, (rows, rows), 0)
    earlier = jnp.dot(
        jnp.where(below, 1.0, 0.0).astype(BF16), (chosen[0] + chosen[1]).astype(BF16), preferred_element_type=F32
    )
    limits = limits_ref[...].astype(F32)
    columns = []
    slots = []
    weights = []
    for k in range(TOP):
        rank = jnp.sum(chosen[k] * earlier, axis=1, keepdims=True)
        limit = jnp.sum(chosen[k] * limits, axis=1, keepdims=True)
        slots.append(index[k] * most + rank)
        columns += [index[k], rank]
        weights.append(jnp.where(rank < limit, given[:, TOP + k : TOP + k + 1], 0.0))
    for weight in weights:
        first = weight.astype(BF16).astype(F32)
        second = (weight - first).astype(BF16).astype(F32)
        columns += [first, second, weight - first - second]
    lane = lax.broadcasted_iota(jnp.int32, (rows, LANES), 1)
    table = jnp.zeros((rows, LANES), F32)
    for number, column in enumerate(columns):
        table = jnp.where(lane == number + 1, column, table)
    turned = table.T[:META]
    turned = jnp.where(line == 0, docs_ref[...].astype(F32), turned).astype(BF16)
    slots_ref[...] = jnp.where(lane == 0, slots[0], jnp.where(lane == 1, slots[1], -1.0))
    stores = []
    for turn in order:
        packed[turn, TOP_ROWS * rows :, :rows] = turned
        packed[turn, TOP_ROWS * rows :, rows:] = jnp.zeros((META, part - rows), BF16)
        for which in range(TOP_ROWS):
            loads[turn, which].wait()
        stores.append(pltpu.make_async_copy(packed.at[turn], out_refs[turn], store_sems.at[turn]))
        stores[-1].start()
    for store in stores:
        store.wait()


TOP_ROWS = 3
VMEM_BYTES = 65400 * 1024
ANYWHERE = pl.BlockSpec(memory_space=pl.ANY)


def most_of(rows, experts):
    return max(2, 3 * rows * TOP // (2 * experts))


def pack(queries, keys, values, doc_ids, expert_index, gates, capacity, owners):
    rows, width = queries.shape[1:]
    part = width // owners
    deep = TOP_ROWS * rows + META
    small = (doc_ids, expert_index[0].T, gates[0].T, capacity[None, :])
    result = pl.pallas_call(
        functools.partial(pack_kernel, owners),
        out_shape=[jax.ShapeDtypeStruct((deep, part), BF16)] * owners + [jax.ShapeDtypeStruct((rows, LANES), F32)],
        in_specs=[ANYWHERE] * 7,
        out_specs=[ANYWHERE] * owners + [pl.BlockSpec(memory_space=pltpu.VMEM)],
        scratch_shapes=[pltpu.VMEM(array.shape, array.dtype) for array in small]
        + [
            pltpu.VMEM((owners, deep, part), BF16),
            pltpu.SemaphoreType.DMA((owners, TOP_ROWS)),
            pltpu.SemaphoreType.DMA((4,)),
            pltpu.SemaphoreType.DMA((owners,)),
        ],
        compiler_params=pltpu.CompilerParams(vmem_limit_bytes=VMEM_BYTES),
        name="pack_by_heads",
    )(queries, keys, values, *small)
    return result[:owners], result[owners]


def attend_kernel(most, count, *refs):
    in_refs, out_refs = refs[:count], refs[count : 2 * count]
    queries, keys, values, wide_values, docs, slots_of, routed, load_sems, store_sems = refs[2 * count :]
    me = lax.axis_index("expert")
    experts = count
    part = queries.shape[2]
    rows = keys.shape[1]
    reach = keys.shape[0] - count
    heads = part // HEAD_DIM
    factor = math.log2(math.e) / math.sqrt(HEAD_DIM)
    loads = []
    for turn in range(count):
        source = me ^ turn
        loads += [
            pltpu.make_async_copy(
                in_refs[turn].at[pl.ds(2 * rows, rows + META)], values.at[reach + source], load_sems.at[turn, 0]
            ),
            pltpu.make_async_copy(in_refs[turn].at[pl.ds(rows, rows)], keys.at[reach + source], load_sems.at[turn, 1]),
            pltpu.make_async_copy(in_refs[turn].at[pl.ds(0, rows)], queries.at[source], load_sems.at[turn, 2]),
        ]
    for load in loads[0::3] + loads[1::3] + loads[2::3]:
        load.start()
    for number in range(reach):
        keys[number] = jnp.zeros((rows, part), BF16)
        for head in range(heads):
            wide_values[head, number] = jnp.zeros((rows, 2 * HEAD_DIM), BF16)
        docs[number] = jnp.full((8, rows), -1.0, F32)
    for load in loads[0::3]:
        load.wait()

    @pl.loop(reach, reach + count, unroll=True)
    def _(number):
        for head in range(heads):
            wide_values[head, number, :, :HEAD_DIM] = values[number, :rows, head * HEAD_DIM : (head + 1) * HEAD_DIM]
            wide_values[head, number, :, HEAD_DIM:] = jnp.ones((rows, HEAD_DIM), BF16)
        meta = values[number, rows:, :rows].astype(F32)
        docs[number] = jnp.broadcast_to(meta[0:1], (8, rows))
        for k in range(TOP):
            slots_of[number, k : k + 1] = meta[1 + 2 * k : 2 + 2 * k] * most + meta[2 + 2 * k : 3 + 2 * k]

    for load in loads[1::3] + loads[2::3]:
        load.wait()
    lower = lax.broadcasted_iota(jnp.int32, (rows, rows), 1) <= lax.broadcasted_iota(jnp.int32, (rows, rows), 0)
    slot_at = lax.broadcasted_iota(jnp.int32, (experts * most, rows), 0).astype(F32)
    nothing = jnp.zeros((rows, rows), BF16)

    def one_pair(pair):
        at = pair * 2
        allowed = []
        for side in range(2):
            square = jnp.broadcast_to(docs[at + side + reach, 0:1], (rows, rows))
            query_docs = square.T
            masks = []
            for step in range(reach):
                key_docs = docs[at + side + step, 0:1]
                if step == 0:
                    key_docs = jnp.where(lower, square, key_docs)
                masks.append(query_docs == key_docs)
            allowed.append(masks)
        done = []
        for head in range(heads):
            lanes = slice(head * HEAD_DIM, (head + 1) * HEAD_DIM)
            query = queries[pl.ds(at, 2), :, lanes].reshape(2 * rows, HEAD_DIM)
            key = keys[pl.ds(at, reach + 2), :, lanes].reshape((reach + 2) * rows, HEAD_DIM)
            scores = lax.dot_general(query, key, (((1,), (1,)), ((), ())), preferred_element_type=F32)
            lines = []
            for side in range(2):
                here = scores[side * rows : (side + 1) * rows]
                cut = [here[:, (side + step) * rows : (side + step + 1) * rows] for step in range(reach + 1)]
                cut = [jnp.where(lower, cut[reach], cut[0])] + cut[1:reach]
                cut = [jnp.where(mask, score, -1e30) for mask, score in zip(allowed[side], cut)]
                highest = jnp.max(functools.reduce(jnp.maximum, cut), axis=1, keepdims=True)
                expo = [jnp.exp2((score - highest) * factor) for score in cut]
                last = jnp.where(lower, expo[0], 0.0).astype(BF16)
                expo = [jnp.where(lower, 0.0, expo[0]).astype(BF16)] + [e.astype(BF16) for e in expo[1:]] + [last]
                lines.append(jnp.concatenate([nothing] * side + expo + [nothing] * (1 - side), axis=1))
            weight = jnp.concatenate(lines, axis=0)
            value = wide_values[head, pl.ds(at, reach + 2)].reshape((reach + 2) * rows, 2 * HEAD_DIM)
            result = jnp.dot(weight, value, preferred_element_type=F32)
            done.append((result[:, :HEAD_DIM] / result[:, HEAD_DIM:]).astype(BF16))
        attended = jnp.concatenate(done, axis=1)
        for side in range(2):
            slots = slots_of[at + side + reach]
            picks = (slot_at == slots[0:1]) | (slot_at == slots[1:2])
            picks = jnp.where(picks, 1.0, 0.0).astype(BF16)
            sent = jnp.dot(picks, attended[side * rows : (side + 1) * rows], preferred_element_type=F32).astype(BF16)
            for expert in range(experts):
                routed[expert, at + side] = sent[expert * most : (expert + 1) * most]

    half = count // 2
    stores = []
    for group in range(2):
        pl.loop(group * half // 2, (group + 1) * half // 2, unroll=True)(one_pair)
        for turn in range(count):
            some = pl.ds(group * half, half)
            stores.append(
                pltpu.make_async_copy(routed.at[me ^ turn, some], out_refs[turn].at[some], store_sems.at[turn, group])
            )
            stores[-1].start()
    for store in stores:
        store.wait()


def attend(gathered, most):
    count = len(gathered)
    deepest, part = gathered[0].shape
    rows = (deepest - META) // TOP_ROWS
    reach = WINDOW // rows
    total = reach + count
    return pl.pallas_call(
        functools.partial(attend_kernel, most, count),
        out_shape=[jax.ShapeDtypeStruct((count, most, part), BF16)] * count,
        in_specs=[ANYWHERE] * count,
        out_specs=[ANYWHERE] * count,
        scratch_shapes=[
            pltpu.VMEM((count, rows, part), BF16),
            pltpu.VMEM((total, rows, part), BF16),
            pltpu.VMEM((total, rows + META, part), BF16),
            pltpu.VMEM((part // HEAD_DIM, total, rows, 2 * HEAD_DIM), BF16),
            pltpu.VMEM((total, 8, rows), F32),
            pltpu.VMEM((total, 8, rows), F32),
            pltpu.VMEM((count, count, most, part), BF16),
            pltpu.SemaphoreType.DMA((count, 3)),
            pltpu.SemaphoreType.DMA((count, 2)),
        ],
        compiler_params=pltpu.CompilerParams(vmem_limit_bytes=VMEM_BYTES),
        name="attend_and_route",
    )(*gathered)


def expert_kernel(pieces, blocks, gain_ref, *refs):
    row_refs, meta_refs, refs = refs[:blocks], refs[blocks : 2 * blocks], refs[2 * blocks :]
    gate_refs, up_refs, down_refs = refs[:pieces], refs[pieces : 2 * pieces], refs[2 * pieces : 3 * pieces]
    refs = refs[3 * pieces :]
    out_refs, refs = refs[:blocks], refs[blocks:]
    held_rows, meta_all, gate_all, up_all, down_all, normed, hidden, answers = refs[:8]
    sems, row_sems, store_sems = refs[8:]
    parts, count, part = held_rows.shape
    most = answers.shape[1]
    wide = gate_all.shape[3]
    width = parts * part
    mine, expert = lax.axis_index("dp"), lax.axis_index("expert")
    loads = []
    for turn in range(blocks):
        source = expert ^ turn
        loads += [
            pltpu.make_async_copy(row_refs[turn], held_rows.at[source], row_sems.at[turn, 0]),
            pltpu.make_async_copy(
                meta_refs[turn].at[pl.ds(meta_refs[turn].shape[0] - META, META)], meta_all.at[source], row_sems.at[turn, 1]
            ),
        ]

    def tile_copies(step):
        tile = pl.ds(pl.multiple_of((mine ^ step) * wide, wide), wide)
        found = []
        for which, (held, weights) in enumerate(((gate_all, gate_refs), (up_all, up_refs))):
            for number in range(pieces):
                source, target = weights[number].at[0, :, tile], held.at[step, mine ^ number]
                found.append(pltpu.make_async_copy(source, target, sems.at[which, step, number]))
        return found

    def down_copy(step):
        return pltpu.make_async_copy(down_refs[step].at[0], down_all.at[step], sems.at[2, 0, step])

    for load in loads:
        load.start()
    for load in loads:
        load.wait()
    for step in range(pieces):
        for copy in tile_copies(step):
            copy.start()
    for step in range(pieces):
        down_copy(step).start()

    squares = jnp.zeros((count, part), F32)
    for number in range(parts):
        held = held_rows[number].astype(F32)
        squares = squares + held * held
    inverse = lax.rsqrt(jnp.sum(squares, axis=1, keepdims=True) / width + 1e-05)
    for number in range(parts):
        lanes = slice(number * part, (number + 1) * part)
        normed[:, lanes] = (held_rows[number].astype(F32) * inverse * gain_ref[:, lanes]).astype(BF16)

    @pl.loop(0, pieces)
    def _(step):
        for copy in tile_copies(step):
            copy.wait()
        held = normed[...]
        gate = jnp.dot(held, gate_all[step].reshape(width, wide), preferred_element_type=F32)
        up = jnp.dot(held, up_all[step].reshape(width, wide), preferred_element_type=F32)
        hidden[step] = (gate / (1.0 + jnp.exp(-gate)) * up).astype(BF16)

    for piece in range(pieces):
        down_copy(piece).wait()

    rows = LANES
    slot_of = lax.broadcasted_iota(jnp.int32, (most, rows), 0).astype(F32) + (expert * most).astype(F32)
    weights, firsts = [], []
    for number in range(blocks):
        meta = meta_all[number, :, :rows].astype(F32)
        total = jnp.zeros((most, rows), F32)
        for k in range(TOP):
            slot = meta[1 + 2 * k : 2 + 2 * k] * most + meta[2 + 2 * k : 3 + 2 * k]
            at = 1 + 2 * TOP + 3 * k
            weight = meta[at : at + 1] + meta[at + 1 : at + 2] + meta[at + 2 : at + 3]
            total = total + jnp.where(slot_of == slot, weight, 0.0)
            if k == 0:
                firsts.append(jnp.sum(jnp.where(slot_of == slot, 1.0, 0.0), axis=1, keepdims=True))
        weights.append(jnp.sum(total, axis=1, keepdims=True))
    weight = jnp.concatenate(weights, axis=0)
    first = jnp.concatenate(firsts, axis=0)

    stores = []
    for number in range(parts):
        lanes = slice(number * part, (number + 1) * part)
        result = jnp.zeros((count, part), F32)
        for piece in range(pieces):
            result = result + jnp.dot(hidden[piece], down_all[piece, :, lanes], preferred_element_type=F32)
        result = result.astype(BF16).astype(F32) * weight
        result = (held_rows[number].astype(F32) * first + result).astype(BF16)
        for source in range(blocks):
            answers[source, :, lanes] = result[source * most : (source + 1) * most]
        if number % 2 == 1:
            for turn in range(blocks):
                some = pl.ds((number - 1) * part, 2 * part)
                stores.append(
                    pltpu.make_async_copy(
                        answers.at[expert ^ turn, :, some], out_refs[turn].at[:, some], store_sems.at[turn, number // 2]
                    )
                )
                stores[-1].start()
    for store in stores:
        store.wait()


def run_expert(rows, gathered, gain, gates, ups, downs, most):
    blocks = len(rows)
    count, part = rows[0].shape
    width = blocks * part
    pieces = len(downs)
    wide = downs[1].shape[1]
    deep = width // pieces
    return pl.pallas_call(
        functools.partial(expert_kernel, pieces, blocks),
        out_shape=[jax.ShapeDtypeStruct((most, width), BF16)] * blocks,
        in_specs=[pl.BlockSpec(memory_space=pltpu.VMEM)]
        + [ANYWHERE] * (2 * blocks + 3 * pieces),
        out_specs=[ANYWHERE] * blocks,
        scratch_shapes=[
            pltpu.VMEM((blocks, count, part), BF16),
            pltpu.VMEM((blocks, META, part), BF16),
            pltpu.VMEM((pieces, pieces, deep, wide), BF16),
            pltpu.VMEM((pieces, pieces, deep, wide), BF16),
            pltpu.VMEM((pieces, wide, width), BF16),
            pltpu.VMEM((count, width), BF16),
            pltpu.VMEM((pieces, count, wide), BF16),
            pltpu.VMEM((blocks, most, width), BF16),
            pltpu.SemaphoreType.DMA((3, pieces, pieces)),
            pltpu.SemaphoreType.DMA((blocks, 2)),
            pltpu.SemaphoreType.DMA((blocks, blocks // 2)),
        ],
        compiler_params=pltpu.CompilerParams(vmem_limit_bytes=VMEM_BYTES),
        name="expert_rows",
    )(gain[None, :], *rows, *gathered, *gates, *ups, *downs)


def combine_kernel(blocks, slots_ref, own_ref, *refs):
    row_refs, out_ref, own, slots, sems = refs[: blocks - 1], *refs[blocks - 1 :]
    loads = [
        pltpu.make_async_copy(slots_ref, slots, sems.at[0]),
        pltpu.make_async_copy(own_ref, own, sems.at[1]),
    ]
    for load in loads:
        load.start()
    most = own.shape[0]
    rows = slots.shape[0]
    column = lax.broadcasted_iota(jnp.int32, (rows, blocks * most), 1)
    slot_of = (((column // most) ^ lax.axis_index("expert")) * most + column % most).astype(F32)
    loads[0].wait()
    picks = (slot_of == slots[:, 0:1]) | (slot_of == slots[:, 1:2])
    picks = jnp.where(picks, 1.0, 0.0).astype(BF16)
    loads[1].wait()
    held = jnp.concatenate([own[...]] + [ref[...] for ref in row_refs], axis=0)
    out_ref[0] = jnp.dot(picks, held, preferred_element_type=F32).astype(BF16)


def combine(returned, slots):
    blocks = len(returned)
    most, width = returned[0].shape
    vmem = pl.BlockSpec(memory_space=pltpu.VMEM)
    return pl.pallas_call(
        functools.partial(combine_kernel, blocks),
        out_shape=jax.ShapeDtypeStruct((1, slots.shape[0], width), BF16),
        in_specs=[pl.BlockSpec(memory_space=pltpu.HBM)] * 2 + [vmem] * (blocks - 1),
        out_specs=vmem,
        scratch_shapes=[
            pltpu.VMEM(returned[0].shape, BF16),
            pltpu.VMEM(slots.shape, F32),
            pltpu.SemaphoreType.DMA((2,)),
        ],
        compiler_params=pltpu.CompilerParams(vmem_limit_bytes=24 * 1024 * 1024),
        name="combine_choices",
    )(slots, *returned)


def flipped(block, axis, bits):
    return lax.ppermute(block, axis, [(i, i ^ bits) for i in range(lax.axis_size(axis))])


def exchange(blocks):
    count = len(blocks)
    moved = {turn: flipped(blocks[turn], "expert", turn) for turn in range(count - 1, 0, -1)}
    return [blocks[0]] + [moved[turn] for turn in range(1, count)]


def per_device(
    queries,
    keys,
    values,
    doc_ids,
    expert_index,
    gates,
    capacity,
    norm_gain,
    gate_weight,
    up_weight,
    down_weight,
):
    rows, width = queries.shape[1:]
    experts = lax.axis_size("expert")
    most = most_of(rows, experts)
    over = lax.axis_size("dp")
    weights = [gate_weight, up_weight, down_weight]
    gate, up, down = ({0: block} for block in weights)
    for number in range(2, over, 2):
        gate[number] = flipped(gate_weight, "dp", number)
    packed, slots = pack(queries, keys, values, doc_ids, expert_index, gates, capacity, experts)
    gathered = exchange(packed)
    gathered, gate, up, down = lax.optimization_barrier((gathered, gate, up, down))
    for pieces in (gate, up, down):
        for number in list(pieces):
            pieces[number + 1] = flipped(pieces[number], "dp", 1)
    for number in range(2, over, 2):
        up[number] = flipped(up_weight, "dp", number)
    routed = list(attend(gathered, most))
    routed, gate, up, down = lax.optimization_barrier((routed, gate, up, down))
    for number in range(2, over, 2):
        down[number] = flipped(down[0], "dp", number)
    received = exchange(routed)
    received, up, down = lax.optimization_barrier((received, up, down))
    for pieces in (up, down):
        for number in range(2, over, 2):
            pieces[number + 1] = flipped(pieces[number], "dp", 1)
    gate, up, down = ([pieces[number] for number in range(over)] for pieces in (gate, up, down))
    received = [block.reshape(experts * most, width // experts) for block in received]
    answered = run_expert(received, gathered, norm_gain, gate, up, down, most)
    return combine(exchange(answered), slots)


def by_heads(mesh, queries, gate_weight):
    over, experts = mesh.shape["dp"], mesh.shape["expert"]
    rows, width = queries.shape[1] // experts, queries.shape[2]
    hidden = gate_weight.shape[2]
    return (
        width % (experts * HEAD_DIM) == 0
        and rows == LANES
        and WINDOW % rows == 0
        and experts % 4 == 0
        and experts & (experts - 1) == 0
        and width // experts > rows
        and (width // over) % (width // experts) == 0
        and hidden % (over * LANES) == 0
        and most_of(rows, experts) % 16 == 0
        and over > 2
        and over & (over - 1) == 0
        and queries.shape[0] == over
        and gate_weight.shape[0] == experts
    )


def solution(mesh):
    placed = (
        P("dp", "expert", None),
        P("dp", "expert", None),
        P("dp", "expert", None),
        P("dp", "expert"),
        P("dp", "expert", None),
        P("dp", "expert", None),
        P(),
        P(),
        P("expert", "dp", None),
        P("expert", "dp", None),
        P("expert", "dp", None),
    )

    def layer(*arrays):
        step = per_device if by_heads(mesh, arrays[0], arrays[8]) else per_device_general
        return jax.shard_map(
            step, mesh=mesh, in_specs=placed, out_specs=P("dp", "expert", None), check_vma=False
        )(*arrays)

    return layer
```

```python
import functools
import math

import jax
import jax.numpy as jnp
from jax import lax
from jax.experimental import pallas as pl
from jax.experimental.pallas import tpu as pltpu
from jax.sharding import PartitionSpec as P

HEAD_DIM = 128
TOP = 2
WINDOW = 512
META = 16
LANES = 128
F32 = jnp.float32
BF16 = jnp.bfloat16


def shifted_2(block, axis, distance):
    devices = range(lax.axis_size(axis))
    route = [(i - distance, i) for i in devices if i - distance in devices]
    return lax.ppermute(block, axis, route)


def attend_local(queries, key_rows, value_rows, query_docs, key_docs, query_start, key_start):
    rows_dev, width = queries.shape
    heads = width // HEAD_DIM
    q_block = min(512, rows_dev)
    before = key_rows.shape[0] - rows_dev

    def one_block(number):
        begin = number * q_block
        query_part = queries.reshape(q_block, heads, HEAD_DIM)
        key_part = key_rows.reshape(before + q_block, heads, HEAD_DIM)
        value_part = value_rows.reshape(before + q_block, heads, HEAD_DIM)
        query_pos = query_start + begin + jnp.arange(q_block, dtype=jnp.int32)
        key_pos = key_start + begin + jnp.arange(before + q_block, dtype=jnp.int32)
        allowed = (key_pos[None, :] <= query_pos[:, None]) & (
            key_pos[None, :] > query_pos[:, None] - WINDOW
        )
        allowed = allowed & (key_pos[None, :] >= 0) & (key_docs[None, :] == query_docs[:, None])
        scores = jnp.einsum(
            "qhd,khd->hqk", query_part, key_part, preferred_element_type=jnp.float32
        ) * (1.0 / math.sqrt(HEAD_DIM))
        scores = jnp.where(allowed[None], scores, -1e30)
        highest = jnp.max(scores, axis=-1, keepdims=True)
        expo = jnp.exp(scores - highest)
        probs = (expo / jnp.sum(expo, axis=-1, keepdims=True)).astype(jnp.bfloat16)
        result = jnp.einsum("hqk,khd->qhd", probs, value_part, preferred_element_type=jnp.float32)
        return result.reshape(q_block, width).astype(jnp.bfloat16)

    blocks = lax.map(one_block, jnp.arange(rows_dev // q_block, dtype=jnp.int32))
    return blocks.reshape(rows_dev, width)


def per_device_general(
    queries,
    keys,
    values,
    doc_ids,
    expert_index,
    gates,
    capacity,
    norm_gain,
    gate_weight,
    up_weight,
    down_weight,
):
    rows_dev = queries.shape[1]
    width = queries.shape[2]
    reach_back = (WINDOW - 1) // rows_dev + 1
    own_pair = jnp.stack([keys[0], values[0]], axis=0)
    own_docs = doc_ids[0].astype(jnp.bfloat16)
    earlier = []
    current = (own_pair, own_docs)
    for number in range(reach_back):
        current = shifted_2((current[0], current[1]), "expert", 1)
        earlier.insert(0, current)
    pair_all = jnp.concatenate([shifted[0] for shifted in earlier] + [own_pair], axis=1)
    docs_all = jnp.concatenate([shifted[1] for shifted in earlier] + [own_docs], axis=0)
    position = lax.axis_index("expert")
    attended = attend_local(
        queries[0],
        pair_all[0],
        pair_all[1],
        own_docs,
        docs_all,
        position * rows_dev,
        (position - reach_back) * rows_dev,
    )
    flat_att = attended.astype(jnp.float32)
    normed = (
        flat_att
        * lax.rsqrt(jnp.mean(flat_att * flat_att, axis=-1, keepdims=True) + 1e-05)
        * norm_gain
    ).astype(jnp.bfloat16)
    experts = lax.axis_size("expert")
    most = max(2, 3 * rows_dev * TOP // (2 * experts))
    chosen_flat = expert_index[0].reshape(-1)
    onehot = (chosen_flat[:, None] == jnp.arange(experts, dtype=jnp.int32)[None, :]).astype(
        jnp.int32
    )
    ranks = jnp.sum(onehot * (jnp.cumsum(onehot, axis=0) - 1), axis=1)
    limits = jnp.sum(onehot * capacity[None, :], axis=1)
    kept = ranks < limits
    slot = jnp.where(kept, chosen_flat * most + ranks, experts * most)
    token_of = jnp.arange(rows_dev * TOP, dtype=jnp.int32) // TOP
    slot_token = jnp.full((experts * most,), -1, jnp.int32).at[slot].set(token_of, mode="drop")
    filled = slot_token >= 0
    outgoing = jnp.where(
        filled[:, None], normed[jnp.maximum(slot_token, 0)], jnp.zeros((), jnp.bfloat16)
    )
    outgoing = outgoing.reshape(experts, most, width)
    received = lax.all_to_all(outgoing, "expert", split_axis=0, concat_axis=0, tiled=True)
    sources = received.shape[0]
    flat_rows = received.reshape(sources * most, width)
    columns = flat_rows
    gate_sum = jnp.dot(
        columns,
        lax.all_gather(gate_weight, "dp", axis=1, tiled=True)[0],
        preferred_element_type=jnp.float32,
    )
    up_sum = jnp.dot(
        columns,
        lax.all_gather(up_weight, "dp", axis=1, tiled=True)[0],
        preferred_element_type=jnp.float32,
    )
    hidden = (jax.nn.silu(gate_sum) * up_sum).astype(jnp.bfloat16)
    columns = hidden
    result = jnp.dot(
        columns,
        lax.all_gather(down_weight, "dp", axis=1, tiled=True)[0],
        preferred_element_type=jnp.float32,
    )
    answered = result.astype(jnp.bfloat16).reshape(sources, most, width)
    returned = lax.all_to_all(answered, "expert", split_axis=0, concat_axis=0, tiled=True)
    back_flat = returned.reshape(experts * most, width)
    picked = back_flat[jnp.minimum(slot, experts * most - 1)].reshape(rows_dev, TOP, width)
    weight = jnp.where(kept, gates[0].reshape(-1), 0.0).reshape(rows_dev, TOP)
    combined = flat_att
    for which in range(TOP):
        combined = combined + picked[:, which].astype(jnp.float32) * weight[:, which : which + 1]
    return combined.astype(jnp.bfloat16)[None]


def pack_kernel(owners, q_ref, k_ref, v_ref, *refs):
    given, out_refs, slots_ref = refs[:4], refs[4 : 4 + owners], refs[4 + owners]
    small, held, packed, sems, store_sems = refs[5 + owners : 9 + owners], *refs[9 + owners :]
    rows = q_ref.shape[1]
    part = packed.shape[2]
    me = lax.axis_index("expert")
    order = list(range(owners // 2, owners)) + list(range(owners // 2))
    fetches = [pltpu.make_async_copy(given[i], small[i], sems.at[i]) for i in range(4)]
    loads = [
        pltpu.make_async_copy(ref.at[0], held.at[which], sems.at[4 + which])
        for which, ref in enumerate((q_ref, k_ref, v_ref))
    ]
    for fetch in fetches + loads:
        fetch.start()
    for fetch in fetches:
        fetch.wait()
    docs_ref, index_ref, gates_ref, limits_ref = small
    experts = limits_ref.shape[1]
    most = most_of(rows, experts)
    line = lax.broadcasted_iota(jnp.int32, (META, rows), 0)
    given = jnp.zeros((META, rows), F32)
    for k in range(TOP):
        given = jnp.where(line == k, index_ref[k : k + 1].astype(F32), given)
        given = jnp.where(line == TOP + k, gates_ref[k : k + 1], given)
    given = jnp.concatenate([given, jnp.zeros((rows - META, rows), F32)], axis=0).T
    index = [given[:, k : k + 1] for k in range(TOP)]
    names = lax.broadcasted_iota(jnp.int32, (rows, experts), 1).astype(F32)
    chosen = [jnp.where(index[k] == names, 1.0, 0.0) for k in range(TOP)]
    below = lax.broadcasted_iota(jnp.int32, (rows, rows), 1) < lax.broadcasted_iota(jnp.int32, (rows, rows), 0)
    earlier = jnp.dot(
        jnp.where(below, 1.0, 0.0).astype(BF16), (chosen[0] + chosen[1]).astype(BF16), preferred_element_type=F32
    )
    limits = limits_ref[...].astype(F32)
    columns = []
    slots = []
    weights = []
    for k in range(TOP):
        rank = jnp.sum(chosen[k] * earlier, axis=1, keepdims=True)
        limit = jnp.sum(chosen[k] * limits, axis=1, keepdims=True)
        slots.append(index[k] * most + rank)
        columns += [index[k], rank]
        weights.append(jnp.where(rank < limit, given[:, TOP + k : TOP + k + 1], 0.0))
    for weight in weights:
        first = weight.astype(BF16).astype(F32)
        second = (weight - first).astype(BF16).astype(F32)
        columns += [first, second, weight - first - second]
    lane = lax.broadcasted_iota(jnp.int32, (rows, LANES), 1)
    table = jnp.zeros((rows, LANES), F32)
    for number, column in enumerate(columns):
        table = jnp.where(lane == number + 1, column, table)
    turned = table.T[:META]
    turned = jnp.where(line == 0, docs_ref[...].astype(F32), turned).astype(BF16)
    slots_ref[...] = jnp.where(lane == 0, slots[0], jnp.where(lane == 1, slots[1], -1.0))
    for load in loads:
        load.wait()
    stores = []
    for turn in order:
        lanes = pl.ds(pl.multiple_of((me ^ turn) * part, part), part)
        for which in range(TOP_ROWS):
            packed[turn, which * rows : (which + 1) * rows, :] = held[which, :, lanes]
        packed[turn, TOP_ROWS * rows :, :rows] = turned
        packed[turn, TOP_ROWS * rows :, rows:] = jnp.zeros((META, part - rows), BF16)
        stores.append(pltpu.make_async_copy(packed.at[turn], out_refs[turn], store_sems.at[turn]))
        stores[-1].start()
    for store in stores:
        store.wait()


TOP_ROWS = 3
VMEM_BYTES = 65400 * 1024
ANYWHERE = pl.BlockSpec(memory_space=pl.ANY)


def most_of(rows, experts):
    return max(2, 3 * rows * TOP // (2 * experts))


def pack(queries, keys, values, doc_ids, expert_index, gates, capacity, owners):
    rows, width = queries.shape[1:]
    part = width // owners
    deep = TOP_ROWS * rows + META
    small = (doc_ids, expert_index[0].T, gates[0].T, capacity[None, :])
    result = pl.pallas_call(
        functools.partial(pack_kernel, owners),
        out_shape=[jax.ShapeDtypeStruct((deep, part), BF16)] * owners + [jax.ShapeDtypeStruct((rows, LANES), F32)],
        in_specs=[ANYWHERE] * 7,
        out_specs=[ANYWHERE] * owners + [pl.BlockSpec(memory_space=pltpu.VMEM)],
        scratch_shapes=[pltpu.VMEM(array.shape, array.dtype) for array in small]
        + [
            pltpu.VMEM((TOP_ROWS, rows, width), BF16),
            pltpu.VMEM((owners, deep, part), BF16),
            pltpu.SemaphoreType.DMA((7,)),
            pltpu.SemaphoreType.DMA((owners,)),
        ],
        compiler_params=pltpu.CompilerParams(vmem_limit_bytes=VMEM_BYTES),
        name="pack_by_heads",
    )(queries, keys, values, *small)
    return result[:owners], result[owners]


def attend_kernel(most, count, *refs):
    in_refs, out_refs = refs[:count], refs[count : 2 * count]
    held, keys, wide_values, docs, slots_of, routed, load_sems, store_sems = refs[2 * count :]
    me = lax.axis_index("expert")
    experts = count
    part = keys.shape[2]
    rows = keys.shape[1]
    reach = keys.shape[0] - count
    heads = part // HEAD_DIM
    factor = math.log2(math.e) / math.sqrt(HEAD_DIM)
    loads = []
    for turn in range(count):
        loads.append(pltpu.make_async_copy(in_refs[turn], held.at[me ^ turn], load_sems.at[turn]))
    for load in loads:
        load.start()
    for number in range(reach):
        keys[number] = jnp.zeros((rows, part), BF16)
        for head in range(heads):
            wide_values[head, number] = jnp.zeros((rows, 2 * HEAD_DIM), BF16)
        docs[number] = jnp.full((8, rows), -1.0, F32)
    for number in range(reach, reach + count):
        for head in range(heads):
            wide_values[head, number, :, HEAD_DIM:] = jnp.ones((rows, HEAD_DIM), BF16)
    for load in loads:
        load.wait()

    @pl.loop(0, count, unroll=True)
    def _(number):
        keys[reach + number] = held[number, rows : 2 * rows]
        for head in range(heads):
            lanes = slice(head * HEAD_DIM, (head + 1) * HEAD_DIM)
            wide_values[head, reach + number, :, :HEAD_DIM] = held[number, 2 * rows : 3 * rows, lanes]
        meta = held[number, TOP_ROWS * rows :, :rows].astype(F32)
        docs[reach + number] = jnp.broadcast_to(meta[0:1], (8, rows))
        for k in range(TOP):
            slots_of[number, k : k + 1] = meta[1 + 2 * k : 2 + 2 * k] * most + meta[2 + 2 * k : 3 + 2 * k]

    lower = lax.broadcasted_iota(jnp.int32, (rows, rows), 1) <= lax.broadcasted_iota(jnp.int32, (rows, rows), 0)
    slot_at = lax.broadcasted_iota(jnp.int32, (experts * most, rows), 0).astype(F32)
    nothing = jnp.zeros((rows, rows), BF16)

    def one_pair(pair):
        at = pair * 2
        allowed = []
        for side in range(2):
            square = jnp.broadcast_to(docs[at + side + reach, 0:1], (rows, rows))
            query_docs = square.T
            masks = []
            for step in range(reach):
                key_docs = docs[at + side + step, 0:1]
                if step == 0:
                    key_docs = jnp.where(lower, square, key_docs)
                masks.append(query_docs == key_docs)
            allowed.append(masks)
        done = []
        for head in range(heads):
            lanes = slice(head * HEAD_DIM, (head + 1) * HEAD_DIM)
            query = held[pl.ds(at, 2), :rows, lanes].reshape(2 * rows, HEAD_DIM)
            key = keys[pl.ds(at, reach + 2), :, lanes].reshape((reach + 2) * rows, HEAD_DIM)
            scores = lax.dot_general(query, key, (((1,), (1,)), ((), ())), preferred_element_type=F32)
            lines = []
            for side in range(2):
                here = scores[side * rows : (side + 1) * rows]
                cut = [here[:, (side + step) * rows : (side + step + 1) * rows] for step in range(reach + 1)]
                cut = [jnp.where(lower, cut[reach], cut[0])] + cut[1:reach]
                cut = [jnp.where(mask, score, -1e30) for mask, score in zip(allowed[side], cut)]
                highest = jnp.max(functools.reduce(jnp.maximum, cut), axis=1, keepdims=True)
                expo = [jnp.exp2((score - highest) * factor) for score in cut]
                last = jnp.where(lower, expo[0], 0.0).astype(BF16)
                expo = [jnp.where(lower, 0.0, expo[0]).astype(BF16)] + [e.astype(BF16) for e in expo[1:]] + [last]
                lines.append(jnp.concatenate([nothing] * side + expo + [nothing] * (1 - side), axis=1))
            weight = jnp.concatenate(lines, axis=0)
            value = wide_values[head, pl.ds(at, reach + 2)].reshape((reach + 2) * rows, 2 * HEAD_DIM)
            result = jnp.dot(weight, value, preferred_element_type=F32)
            done.append((result[:, :HEAD_DIM] / result[:, HEAD_DIM:]).astype(BF16))
        attended = jnp.concatenate(done, axis=1)
        for side in range(2):
            slots = slots_of[at + side]
            picks = (slot_at == slots[0:1]) | (slot_at == slots[1:2])
            picks = jnp.where(picks, 1.0, 0.0).astype(BF16)
            sent = jnp.dot(picks, attended[side * rows : (side + 1) * rows], preferred_element_type=F32).astype(BF16)
            for expert in range(experts):
                routed[expert, at + side] = sent[expert * most : (expert + 1) * most]

    half = count // 2
    stores = []
    for group in range(2):
        pl.loop(group * half // 2, (group + 1) * half // 2, unroll=True)(one_pair)
        for turn in range(count):
            some = pl.ds(group * half, half)
            stores.append(
                pltpu.make_async_copy(routed.at[me ^ turn, some], out_refs[turn].at[some], store_sems.at[turn, group])
            )
            stores[-1].start()
    for store in stores:
        store.wait()


def attend(gathered, most):
    count = len(gathered)
    deepest, part = gathered[0].shape
    rows = (deepest - META) // TOP_ROWS
    reach = WINDOW // rows
    total = reach + count
    return pl.pallas_call(
        functools.partial(attend_kernel, most, count),
        out_shape=[jax.ShapeDtypeStruct((count, most, part), BF16)] * count,
        in_specs=[ANYWHERE] * count,
        out_specs=[ANYWHERE] * count,
        scratch_shapes=[
            pltpu.VMEM((count, deepest, part), BF16),
            pltpu.VMEM((total, rows, part), BF16),
            pltpu.VMEM((part // HEAD_DIM, total, rows, 2 * HEAD_DIM), BF16),
            pltpu.VMEM((total, 8, rows), F32),
            pltpu.VMEM((total, 8, rows), F32),
            pltpu.VMEM((count, count, most, part), BF16),
            pltpu.SemaphoreType.DMA((count,)),
            pltpu.SemaphoreType.DMA((count, 2)),
        ],
        compiler_params=pltpu.CompilerParams(vmem_limit_bytes=VMEM_BYTES),
        name="attend_and_route",
    )(*gathered)


def expert_kernel(pieces, blocks, turns, gain_ref, *refs):
    some = len(turns)
    row_refs, meta_refs, refs = refs[:blocks], refs[blocks : blocks + some], refs[blocks + some :]
    gate_refs, up_refs, down_refs = refs[:pieces], refs[pieces : 2 * pieces], refs[2 * pieces : 3 * pieces]
    refs = refs[3 * pieces :]
    out_refs, refs = refs[:some], refs[some:]
    held_rows, meta_all, gate_all, up_all, down_all, normed, hidden, answers = refs[:8]
    sems, row_sems, store_sems = refs[8:]
    parts, count, part = held_rows.shape
    most = answers.shape[1]
    wide = gate_all.shape[3]
    width = parts * part
    mine, expert = lax.axis_index("dp"), lax.axis_index("expert")
    at = [(expert ^ turn) & (some - 1) for turn in turns]
    first_row = pl.multiple_of(((expert ^ turns[0]) - at[0]) * most, 16)
    loads = []
    for turn in range(blocks):
        rows = row_refs[turn].at[pl.ds(first_row, count)]
        loads.append(pltpu.make_async_copy(rows, held_rows.at[expert ^ turn], row_sems.at[turn, 0]))
    for number in range(some):
        meta = meta_refs[number].at[pl.ds(meta_refs[number].shape[0] - META, META)]
        loads.append(pltpu.make_async_copy(meta, meta_all.at[at[number]], row_sems.at[number, 1]))

    def tile_copies(step):
        tile = pl.ds(pl.multiple_of((mine ^ step) * wide, wide), wide)
        found = []
        for which, (held, weights) in enumerate(((gate_all, gate_refs), (up_all, up_refs))):
            for number in range(pieces):
                source, target = weights[number].at[0, :, tile], held.at[step, mine ^ number]
                found.append(pltpu.make_async_copy(source, target, sems.at[which, step, number]))
        return found

    def down_copy(step):
        return pltpu.make_async_copy(down_refs[step].at[0], down_all.at[step], sems.at[2, 0, step])

    for load in loads:
        load.start()
    for step in range(pieces):
        for copy in tile_copies(step):
            copy.start(priority=1)
    for step in range(pieces):
        down_copy(step).start(priority=1)
    for load in loads:
        load.wait()

    squares = jnp.zeros((count, part), F32)
    for number in range(parts):
        held = held_rows[number].astype(F32)
        squares = squares + held * held
    inverse = lax.rsqrt(jnp.sum(squares, axis=1, keepdims=True) / width + 1e-05)
    for number in range(parts):
        lanes = slice(number * part, (number + 1) * part)
        normed[:, lanes] = (held_rows[number].astype(F32) * inverse * gain_ref[:, lanes]).astype(BF16)

    @pl.loop(0, pieces)
    def _(step):
        for copy in tile_copies(step):
            copy.wait()
        held = normed[...]
        gate = jnp.dot(held, gate_all[step].reshape(width, wide), preferred_element_type=F32)
        up = jnp.dot(held, up_all[step].reshape(width, wide), preferred_element_type=F32)
        hidden[step] = (gate / (1.0 + jnp.exp(-gate)) * up).astype(BF16)

    for piece in range(pieces):
        down_copy(piece).wait()

    rows = LANES
    slot_of = lax.broadcasted_iota(jnp.int32, (most, rows), 0).astype(F32) + (expert * most).astype(F32)
    weights, firsts = [], []
    for number in range(some):
        meta = meta_all[number, :, :rows].astype(F32)
        total = jnp.zeros((most, rows), F32)
        for k in range(TOP):
            slot = meta[1 + 2 * k : 2 + 2 * k] * most + meta[2 + 2 * k : 3 + 2 * k]
            line = 1 + 2 * TOP + 3 * k
            weight = meta[line : line + 1] + meta[line + 1 : line + 2] + meta[line + 2 : line + 3]
            total = total + jnp.where(slot_of == slot, weight, 0.0)
            if k == 0:
                firsts.append(jnp.sum(jnp.where(slot_of == slot, 1.0, 0.0), axis=1, keepdims=True))
        weights.append(jnp.sum(total, axis=1, keepdims=True))
    weight = jnp.concatenate(weights, axis=0)
    first = jnp.concatenate(firsts, axis=0)

    stores = []
    for number in range(parts):
        lanes = slice(number * part, (number + 1) * part)
        result = jnp.zeros((count, part), F32)
        for piece in range(pieces):
            result = result + jnp.dot(hidden[piece], down_all[piece, :, lanes], preferred_element_type=F32)
        result = result.astype(BF16).astype(F32) * weight
        result = (held_rows[number].astype(F32) * first + result).astype(BF16)
        for source in range(some):
            answers[source, :, lanes] = result[source * most : (source + 1) * most]
        if number % 2 == 1:
            columns = pl.ds((number - 1) * part, 2 * part)
            for turn in range(some):
                source, target = answers.at[at[turn], :, columns], out_refs[turn].at[:, columns]
                stores.append(pltpu.make_async_copy(source, target, store_sems.at[turn, number // 2]))
                stores[-1].start()
    for store in stores:
        store.wait()


def run_expert(turns, rows, gathered, gain, gates, ups, downs, most):
    blocks = len(rows)
    count, part = len(turns) * most, rows[0].shape[1]
    width = blocks * part
    pieces = len(downs)
    wide = downs[1].shape[1]
    deep = width // pieces
    return pl.pallas_call(
        functools.partial(expert_kernel, pieces, blocks, turns),
        out_shape=[jax.ShapeDtypeStruct((most, width), BF16)] * len(turns),
        in_specs=[pl.BlockSpec(memory_space=pltpu.VMEM)]
        + [ANYWHERE] * (blocks + len(turns) + 3 * pieces),
        out_specs=[ANYWHERE] * len(turns),
        scratch_shapes=[
            pltpu.VMEM((blocks, count, part), BF16),
            pltpu.VMEM((len(turns), META, part), BF16),
            pltpu.VMEM((pieces, pieces, deep, wide), BF16),
            pltpu.VMEM((pieces, pieces, deep, wide), BF16),
            pltpu.VMEM((pieces, wide, width), BF16),
            pltpu.VMEM((count, width), BF16),
            pltpu.VMEM((pieces, count, wide), BF16),
            pltpu.VMEM((len(turns), most, width), BF16),
            pltpu.SemaphoreType.DMA((3, pieces, pieces)),
            pltpu.SemaphoreType.DMA((blocks, 2)),
            pltpu.SemaphoreType.DMA((blocks, blocks // 2)),
        ],
        compiler_params=pltpu.CompilerParams(vmem_limit_bytes=VMEM_BYTES),
        name="expert_rows",
    )(gain[None, :], *rows, *(gathered[turn] for turn in turns), *gates, *ups, *downs)


def combine_kernel(blocks, slots_ref, own_ref, *refs):
    row_refs, out_ref, own, slots, sems = refs[: blocks - 1], *refs[blocks - 1 :]
    loads = [
        pltpu.make_async_copy(slots_ref, slots, sems.at[0]),
        pltpu.make_async_copy(own_ref, own, sems.at[1]),
    ]
    for load in loads:
        load.start()
    most = own.shape[0]
    rows = slots.shape[0]
    column = lax.broadcasted_iota(jnp.int32, (rows, blocks * most), 1)
    slot_of = (((column // most) ^ lax.axis_index("expert")) * most + column % most).astype(F32)
    loads[0].wait()
    picks = (slot_of == slots[:, 0:1]) | (slot_of == slots[:, 1:2])
    picks = jnp.where(picks, 1.0, 0.0).astype(BF16)
    loads[1].wait()
    held = jnp.concatenate([own[...]] + [ref[...] for ref in row_refs], axis=0)
    out_ref[0] = jnp.dot(picks, held, preferred_element_type=F32).astype(BF16)


def combine(returned, slots):
    blocks = len(returned)
    most, width = returned[0].shape
    vmem = pl.BlockSpec(memory_space=pltpu.VMEM)
    return pl.pallas_call(
        functools.partial(combine_kernel, blocks),
        out_shape=jax.ShapeDtypeStruct((1, slots.shape[0], width), BF16),
        in_specs=[pl.BlockSpec(memory_space=pltpu.HBM)] * 2 + [vmem] * (blocks - 1),
        out_specs=vmem,
        scratch_shapes=[
            pltpu.VMEM(returned[0].shape, BF16),
            pltpu.VMEM(slots.shape, F32),
            pltpu.SemaphoreType.DMA((2,)),
        ],
        compiler_params=pltpu.CompilerParams(vmem_limit_bytes=24 * 1024 * 1024),
        name="combine_choices",
    )(slots, *returned)


def flipped(block, axis, bits):
    return lax.ppermute(block, axis, [(i, i ^ bits) for i in range(lax.axis_size(axis))])


def exchange(blocks):
    count = len(blocks)
    moved = {turn: flipped(blocks[turn], "expert", turn) for turn in range(count - 1, 0, -1)}
    return [blocks[0]] + [moved[turn] for turn in range(1, count)]


def per_device(
    queries,
    keys,
    values,
    doc_ids,
    expert_index,
    gates,
    capacity,
    norm_gain,
    gate_weight,
    up_weight,
    down_weight,
):
    rows, width = queries.shape[1:]
    experts = lax.axis_size("expert")
    half = experts // 2
    most = most_of(rows, experts)
    over = lax.axis_size("dp")
    weights = [gate_weight, up_weight, down_weight]
    gate, up, down = ({0: block} for block in weights)
    for number in range(2, over, 2):
        gate[number] = flipped(gate_weight, "dp", number)
    packed, slots = pack(queries, keys, values, doc_ids, expert_index, gates, capacity, experts)
    gathered = exchange(packed)
    gathered, gate, up, down = lax.optimization_barrier((gathered, gate, up, down))
    for pieces in (gate, up, down):
        for number in list(pieces):
            pieces[number + 1] = flipped(pieces[number], "dp", 1)
    for number in range(2, over, 2):
        up[number] = flipped(up_weight, "dp", number)
    routed = list(attend(gathered, most))
    routed, gate, up, down = lax.optimization_barrier((routed, gate, up, down))
    for number in range(2, over, 2):
        down[number] = flipped(down[0], "dp", number)
    received = exchange(routed)
    received, up, down = lax.optimization_barrier((received, up, down))
    for pieces in (up, down):
        for number in range(2, over, 2):
            pieces[number + 1] = flipped(pieces[number], "dp", 1)
    gate, up, down = ([pieces[number] for number in range(over)] for pieces in (gate, up, down))
    received = [block.reshape(experts * most, width // experts) for block in received]
    answered = []
    for turns in (range(half, experts), range(half)):
        answered = [*run_expert(turns, received, gathered, norm_gain, gate, up, down, most), *answered]
    return combine(exchange(answered), slots)


def by_heads(mesh, queries, gate_weight):
    over, experts = mesh.shape["dp"], mesh.shape["expert"]
    rows, width = queries.shape[1] // experts, queries.shape[2]
    hidden = gate_weight.shape[2]
    return (
        width % (experts * HEAD_DIM) == 0
        and rows == LANES
        and WINDOW % rows == 0
        and experts % 4 == 0
        and experts & (experts - 1) == 0
        and width // experts > rows
        and (width // over) % (width // experts) == 0
        and hidden % (over * LANES) == 0
        and most_of(rows, experts) % 16 == 0
        and over > 2
        and over & (over - 1) == 0
        and queries.shape[0] == over
        and gate_weight.shape[0] == experts
    )


def solution(mesh):
    placed = (
        P("dp", "expert", None),
        P("dp", "expert", None),
        P("dp", "expert", None),
        P("dp", "expert"),
        P("dp", "expert", None),
        P("dp", "expert", None),
        P(),
        P(),
        P("expert", "dp", None),
        P("expert", "dp", None),
        P("expert", "dp", None),
    )

    def layer(*arrays):
        step = per_device if by_heads(mesh, arrays[0], arrays[8]) else per_device_general
        return jax.shard_map(
            step, mesh=mesh, in_specs=placed, out_specs=P("dp", "expert", None), check_vma=False
        )(*arrays)

    return layer
```

```python
import functools
import math

import jax
import jax.numpy as jnp
from jax import lax
from jax.experimental import pallas as pl
from jax.experimental.pallas import tpu as pltpu
from jax.sharding import PartitionSpec as P

HEAD_DIM = 128
TOP = 2
WINDOW = 512
META = 16
LANES = 128
F32 = jnp.float32
BF16 = jnp.bfloat16


def shifted_2(block, axis, distance):
    devices = range(lax.axis_size(axis))
    route = [(i - distance, i) for i in devices if i - distance in devices]
    return lax.ppermute(block, axis, route)


def attend_local(queries, key_rows, value_rows, query_docs, key_docs, query_start, key_start):
    rows_dev, width = queries.shape
    heads = width // HEAD_DIM
    q_block = min(512, rows_dev)
    before = key_rows.shape[0] - rows_dev

    def one_block(number):
        begin = number * q_block
        query_part = queries.reshape(q_block, heads, HEAD_DIM)
        key_part = key_rows.reshape(before + q_block, heads, HEAD_DIM)
        value_part = value_rows.reshape(before + q_block, heads, HEAD_DIM)
        query_pos = query_start + begin + jnp.arange(q_block, dtype=jnp.int32)
        key_pos = key_start + begin + jnp.arange(before + q_block, dtype=jnp.int32)
        allowed = (key_pos[None, :] <= query_pos[:, None]) & (
            key_pos[None, :] > query_pos[:, None] - WINDOW
        )
        allowed = allowed & (key_pos[None, :] >= 0) & (key_docs[None, :] == query_docs[:, None])
        scores = jnp.einsum(
            "qhd,khd->hqk", query_part, key_part, preferred_element_type=jnp.float32
        ) * (1.0 / math.sqrt(HEAD_DIM))
        scores = jnp.where(allowed[None], scores, -1e30)
        highest = jnp.max(scores, axis=-1, keepdims=True)
        expo = jnp.exp(scores - highest)
        probs = (expo / jnp.sum(expo, axis=-1, keepdims=True)).astype(jnp.bfloat16)
        result = jnp.einsum("hqk,khd->qhd", probs, value_part, preferred_element_type=jnp.float32)
        return result.reshape(q_block, width).astype(jnp.bfloat16)

    blocks = lax.map(one_block, jnp.arange(rows_dev // q_block, dtype=jnp.int32))
    return blocks.reshape(rows_dev, width)


def per_device_general(
    queries,
    keys,
    values,
    doc_ids,
    expert_index,
    gates,
    capacity,
    norm_gain,
    gate_weight,
    up_weight,
    down_weight,
):
    rows_dev = queries.shape[1]
    width = queries.shape[2]
    reach_back = (WINDOW - 1) // rows_dev + 1
    own_pair = jnp.stack([keys[0], values[0]], axis=0)
    own_docs = doc_ids[0].astype(jnp.bfloat16)
    earlier = []
    current = (own_pair, own_docs)
    for number in range(reach_back):
        current = shifted_2((current[0], current[1]), "expert", 1)
        earlier.insert(0, current)
    pair_all = jnp.concatenate([shifted[0] for shifted in earlier] + [own_pair], axis=1)
    docs_all = jnp.concatenate([shifted[1] for shifted in earlier] + [own_docs], axis=0)
    position = lax.axis_index("expert")
    attended = attend_local(
        queries[0],
        pair_all[0],
        pair_all[1],
        own_docs,
        docs_all,
        position * rows_dev,
        (position - reach_back) * rows_dev,
    )
    flat_att = attended.astype(jnp.float32)
    normed = (
        flat_att
        * lax.rsqrt(jnp.mean(flat_att * flat_att, axis=-1, keepdims=True) + 1e-05)
        * norm_gain
    ).astype(jnp.bfloat16)
    experts = lax.axis_size("expert")
    most = max(2, 3 * rows_dev * TOP // (2 * experts))
    chosen_flat = expert_index[0].reshape(-1)
    onehot = (chosen_flat[:, None] == jnp.arange(experts, dtype=jnp.int32)[None, :]).astype(
        jnp.int32
    )
    ranks = jnp.sum(onehot * (jnp.cumsum(onehot, axis=0) - 1), axis=1)
    limits = jnp.sum(onehot * capacity[None, :], axis=1)
    kept = ranks < limits
    slot = jnp.where(kept, chosen_flat * most + ranks, experts * most)
    token_of = jnp.arange(rows_dev * TOP, dtype=jnp.int32) // TOP
    slot_token = jnp.full((experts * most,), -1, jnp.int32).at[slot].set(token_of, mode="drop")
    filled = slot_token >= 0
    outgoing = jnp.where(
        filled[:, None], normed[jnp.maximum(slot_token, 0)], jnp.zeros((), jnp.bfloat16)
    )
    outgoing = outgoing.reshape(experts, most, width)
    received = lax.all_to_all(outgoing, "expert", split_axis=0, concat_axis=0, tiled=True)
    sources = received.shape[0]
    flat_rows = received.reshape(sources * most, width)
    columns = flat_rows
    gate_sum = jnp.dot(
        columns,
        lax.all_gather(gate_weight, "dp", axis=1, tiled=True)[0],
        preferred_element_type=jnp.float32,
    )
    up_sum = jnp.dot(
        columns,
        lax.all_gather(up_weight, "dp", axis=1, tiled=True)[0],
        preferred_element_type=jnp.float32,
    )
    hidden = (jax.nn.silu(gate_sum) * up_sum).astype(jnp.bfloat16)
    columns = hidden
    result = jnp.dot(
        columns,
        lax.all_gather(down_weight, "dp", axis=1, tiled=True)[0],
        preferred_element_type=jnp.float32,
    )
    answered = result.astype(jnp.bfloat16).reshape(sources, most, width)
    returned = lax.all_to_all(answered, "expert", split_axis=0, concat_axis=0, tiled=True)
    back_flat = returned.reshape(experts * most, width)
    picked = back_flat[jnp.minimum(slot, experts * most - 1)].reshape(rows_dev, TOP, width)
    weight = jnp.where(kept, gates[0].reshape(-1), 0.0).reshape(rows_dev, TOP)
    combined = flat_att
    for which in range(TOP):
        combined = combined + picked[:, which].astype(jnp.float32) * weight[:, which : which + 1]
    return combined.astype(jnp.bfloat16)[None]


def pack_kernel(owners, q_ref, k_ref, v_ref, *refs):
    given, out_refs, slots_ref = refs[:4], refs[4 : 4 + owners], refs[4 + owners]
    small, held, packed, sems, store_sems = refs[5 + owners : 9 + owners], *refs[9 + owners :]
    rows = q_ref.shape[1]
    part = packed.shape[2]
    me = lax.axis_index("expert")
    order = list(range(owners // 2, owners)) + list(range(owners // 2))
    fetches = [pltpu.make_async_copy(given[i], small[i], sems.at[i]) for i in range(4)]
    loads = [
        pltpu.make_async_copy(ref.at[0], held.at[which], sems.at[4 + which])
        for which, ref in enumerate((q_ref, k_ref, v_ref))
    ]
    for fetch in fetches + loads:
        fetch.start()
    for fetch in fetches:
        fetch.wait()
    docs_ref, index_ref, gates_ref, limits_ref = small
    experts = limits_ref.shape[1]
    most = most_of(rows, experts)
    line = lax.broadcasted_iota(jnp.int32, (META, rows), 0)
    given = jnp.zeros((META, rows), F32)
    for k in range(TOP):
        given = jnp.where(line == k, index_ref[k : k + 1].astype(F32), given)
        given = jnp.where(line == TOP + k, gates_ref[k : k + 1], given)
    given = jnp.concatenate([given, jnp.zeros((rows - META, rows), F32)], axis=0).T
    index = [given[:, k : k + 1] for k in range(TOP)]
    names = lax.broadcasted_iota(jnp.int32, (rows, experts), 1).astype(F32)
    chosen = [jnp.where(index[k] == names, 1.0, 0.0) for k in range(TOP)]
    below = lax.broadcasted_iota(jnp.int32, (rows, rows), 1) < lax.broadcasted_iota(jnp.int32, (rows, rows), 0)
    earlier = jnp.dot(
        jnp.where(below, 1.0, 0.0).astype(BF16), (chosen[0] + chosen[1]).astype(BF16), preferred_element_type=F32
    )
    limits = limits_ref[...].astype(F32)
    columns = []
    slots = []
    weights = []
    for k in range(TOP):
        rank = jnp.sum(chosen[k] * earlier, axis=1, keepdims=True)
        limit = jnp.sum(chosen[k] * limits, axis=1, keepdims=True)
        slots.append(index[k] * most + rank)
        columns += [index[k], rank]
        weights.append(jnp.where(rank < limit, given[:, TOP + k : TOP + k + 1], 0.0))
    for weight in weights:
        first = weight.astype(BF16).astype(F32)
        second = (weight - first).astype(BF16).astype(F32)
        columns += [first, second, weight - first - second]
    lane = lax.broadcasted_iota(jnp.int32, (rows, LANES), 1)
    table = jnp.zeros((rows, LANES), F32)
    for number, column in enumerate(columns):
        table = jnp.where(lane == number + 1, column, table)
    turned = table.T[:META]
    turned = jnp.where(line == 0, docs_ref[...].astype(F32), turned).astype(BF16)
    slots_ref[...] = jnp.where(lane == 0, slots[0], jnp.where(lane == 1, slots[1], -1.0))
    for load in loads:
        load.wait()
    stores = []
    for turn in order:
        lanes = pl.ds(pl.multiple_of((me ^ turn) * part, part), part)
        for which in range(TOP_ROWS):
            packed[turn, which * rows : (which + 1) * rows, :] = held[which, :, lanes]
        packed[turn, TOP_ROWS * rows :, :rows] = turned
        packed[turn, TOP_ROWS * rows :, rows:] = jnp.zeros((META, part - rows), BF16)
        stores.append(pltpu.make_async_copy(packed.at[turn], out_refs[turn], store_sems.at[turn]))
        stores[-1].start()
    for store in stores:
        store.wait()


TOP_ROWS = 3
VMEM_BYTES = 65400 * 1024
ANYWHERE = pl.BlockSpec(memory_space=pl.ANY)


def most_of(rows, experts):
    return max(2, 3 * rows * TOP // (2 * experts))


def pack(queries, keys, values, doc_ids, expert_index, gates, capacity, owners):
    rows, width = queries.shape[1:]
    part = width // owners
    deep = TOP_ROWS * rows + META
    small = (doc_ids, expert_index[0].T, gates[0].T, capacity[None, :])
    result = pl.pallas_call(
        functools.partial(pack_kernel, owners),
        out_shape=[jax.ShapeDtypeStruct((deep, part), BF16)] * owners + [jax.ShapeDtypeStruct((rows, LANES), F32)],
        in_specs=[ANYWHERE] * 7,
        out_specs=[ANYWHERE] * owners + [pl.BlockSpec(memory_space=pltpu.VMEM)],
        scratch_shapes=[pltpu.VMEM(array.shape, array.dtype) for array in small]
        + [
            pltpu.VMEM((TOP_ROWS, rows, width), BF16),
            pltpu.VMEM((owners, deep, part), BF16),
            pltpu.SemaphoreType.DMA((7,)),
            pltpu.SemaphoreType.DMA((owners,)),
        ],
        compiler_params=pltpu.CompilerParams(vmem_limit_bytes=VMEM_BYTES),
        name="pack_by_heads",
    )(queries, keys, values, *small)
    return result[:owners], result[owners]


def attend_kernel(most, count, *refs):
    in_refs, out_refs = refs[:count], refs[count : 2 * count]
    held, keys, wide_values, docs, slots_of, routed, load_sems, store_sems = refs[2 * count :]
    me = lax.axis_index("expert")
    experts = count
    part = keys.shape[2]
    rows = keys.shape[1]
    reach = keys.shape[0] - count
    heads = part // HEAD_DIM
    factor = math.log2(math.e) / math.sqrt(HEAD_DIM)
    loads = []
    for turn in range(count):
        loads.append(pltpu.make_async_copy(in_refs[turn], held.at[me ^ turn], load_sems.at[turn]))
    for load in loads:
        load.start()
    for number in range(reach):
        keys[number] = jnp.zeros((rows, part), BF16)
        for head in range(heads):
            wide_values[head, number] = jnp.zeros((rows, 2 * HEAD_DIM), BF16)
        docs[number] = jnp.full((8, rows), -1.0, F32)
    for number in range(reach, reach + count):
        for head in range(heads):
            wide_values[head, number, :, HEAD_DIM:] = jnp.ones((rows, HEAD_DIM), BF16)
    for load in loads:
        load.wait()

    @pl.loop(0, count, unroll=True)
    def _(number):
        keys[reach + number] = held[number, rows : 2 * rows]
        for head in range(heads):
            lanes = slice(head * HEAD_DIM, (head + 1) * HEAD_DIM)
            wide_values[head, reach + number, :, :HEAD_DIM] = held[number, 2 * rows : 3 * rows, lanes]
        meta = held[number, TOP_ROWS * rows :, :rows].astype(F32)
        docs[reach + number] = jnp.broadcast_to(meta[0:1], (8, rows))
        for k in range(TOP):
            slots_of[number, k : k + 1] = meta[1 + 2 * k : 2 + 2 * k] * most + meta[2 + 2 * k : 3 + 2 * k]

    lower = lax.broadcasted_iota(jnp.int32, (rows, rows), 1) <= lax.broadcasted_iota(jnp.int32, (rows, rows), 0)
    slot_at = lax.broadcasted_iota(jnp.int32, (experts * most, rows), 0).astype(F32)
    nothing = jnp.zeros((rows, rows), BF16)

    def one_pair(pair):
        at = pair * 2
        allowed = []
        for side in range(2):
            square = jnp.broadcast_to(docs[at + side + reach, 0:1], (rows, rows))
            query_docs = square.T
            masks = []
            for step in range(reach):
                key_docs = docs[at + side + step, 0:1]
                if step == 0:
                    key_docs = jnp.where(lower, square, key_docs)
                masks.append(query_docs == key_docs)
            allowed.append(masks)
        done = []
        for head in range(heads):
            lanes = slice(head * HEAD_DIM, (head + 1) * HEAD_DIM)
            query = held[pl.ds(at, 2), :rows, lanes].reshape(2 * rows, HEAD_DIM)
            key = keys[pl.ds(at, reach + 2), :, lanes].reshape((reach + 2) * rows, HEAD_DIM)
            scores = lax.dot_general(query, key, (((1,), (1,)), ((), ())), preferred_element_type=F32)
            lines = []
            for side in range(2):
                here = scores[side * rows : (side + 1) * rows]
                cut = [here[:, (side + step) * rows : (side + step + 1) * rows] for step in range(reach + 1)]
                cut = [jnp.where(lower, cut[reach], cut[0])] + cut[1:reach]
                cut = [jnp.where(mask, score, -1e30) for mask, score in zip(allowed[side], cut)]
                highest = jnp.max(functools.reduce(jnp.maximum, cut), axis=1, keepdims=True)
                expo = [jnp.exp2((score - highest) * factor) for score in cut]
                last = jnp.where(lower, expo[0], 0.0).astype(BF16)
                expo = [jnp.where(lower, 0.0, expo[0]).astype(BF16)] + [e.astype(BF16) for e in expo[1:]] + [last]
                lines.append(jnp.concatenate([nothing] * side + expo + [nothing] * (1 - side), axis=1))
            weight = jnp.concatenate(lines, axis=0)
            value = wide_values[head, pl.ds(at, reach + 2)].reshape((reach + 2) * rows, 2 * HEAD_DIM)
            result = jnp.dot(weight, value, preferred_element_type=F32)
            done.append((result[:, :HEAD_DIM] / result[:, HEAD_DIM:]).astype(BF16))
        attended = jnp.concatenate(done, axis=1)
        for side in range(2):
            slots = slots_of[at + side]
            picks = (slot_at == slots[0:1]) | (slot_at == slots[1:2])
            picks = jnp.where(picks, 1.0, 0.0).astype(BF16)
            sent = jnp.dot(picks, attended[side * rows : (side + 1) * rows], preferred_element_type=F32).astype(BF16)
            for expert in range(experts):
                routed[expert, at + side] = sent[expert * most : (expert + 1) * most]

    half = count // 2
    stores = []
    for group in range(2):
        pl.loop(group * half // 2, (group + 1) * half // 2, unroll=True)(one_pair)
        for turn in range(count):
            some = pl.ds(group * half, half)
            stores.append(
                pltpu.make_async_copy(routed.at[me ^ turn, some], out_refs[turn].at[some], store_sems.at[turn, group])
            )
            stores[-1].start()
    for store in stores:
        store.wait()


def attend(gathered, most):
    count = len(gathered)
    deepest, part = gathered[0].shape
    rows = (deepest - META) // TOP_ROWS
    reach = WINDOW // rows
    total = reach + count
    return pl.pallas_call(
        functools.partial(attend_kernel, most, count),
        out_shape=[jax.ShapeDtypeStruct((count, most, part), BF16)] * count,
        in_specs=[ANYWHERE] * count,
        out_specs=[ANYWHERE] * count,
        scratch_shapes=[
            pltpu.VMEM((count, deepest, part), BF16),
            pltpu.VMEM((total, rows, part), BF16),
            pltpu.VMEM((part // HEAD_DIM, total, rows, 2 * HEAD_DIM), BF16),
            pltpu.VMEM((total, 8, rows), F32),
            pltpu.VMEM((total, 8, rows), F32),
            pltpu.VMEM((count, count, most, part), BF16),
            pltpu.SemaphoreType.DMA((count,)),
            pltpu.SemaphoreType.DMA((count, 2)),
        ],
        compiler_params=pltpu.CompilerParams(vmem_limit_bytes=VMEM_BYTES),
        name="attend_and_route",
    )(*gathered)


def expert_kernel(pieces, blocks, turns, gain_ref, *refs):
    some = len(turns)
    row_refs, meta_refs, refs = refs[:blocks], refs[blocks : blocks + some], refs[blocks + some :]
    gate_refs, up_refs, down_refs = refs[:pieces], refs[pieces : 2 * pieces], refs[2 * pieces : 3 * pieces]
    refs = refs[3 * pieces :]
    out_refs, refs = refs[:some], refs[some:]
    held_rows, meta_all, gate_all, up_all, down_all, normed, hidden, answers = refs[:8]
    sems, row_sems, store_sems = refs[8:]
    parts, count, part = held_rows.shape
    most = answers.shape[1]
    wide = gate_all.shape[3]
    width = parts * part
    mine, expert = lax.axis_index("dp"), lax.axis_index("expert")
    at = [(expert ^ turn) & (some - 1) for turn in turns]
    first_row = pl.multiple_of(((expert ^ turns[0]) - at[0]) * most, 16)
    loads = []
    for turn in range(blocks):
        rows = row_refs[turn].at[pl.ds(first_row, count)]
        loads.append(pltpu.make_async_copy(rows, held_rows.at[expert ^ turn], row_sems.at[turn, 0]))
    for number in range(some):
        meta = meta_refs[number].at[pl.ds(meta_refs[number].shape[0] - META, META)]
        loads.append(pltpu.make_async_copy(meta, meta_all.at[at[number]], row_sems.at[number, 1]))

    def tile_copies(step):
        tile = pl.ds(pl.multiple_of((mine ^ step) * wide, wide), wide)
        found = []
        for which, (held, weights) in enumerate(((gate_all, gate_refs), (up_all, up_refs))):
            for number in range(pieces):
                source, target = weights[number].at[0, :, tile], held.at[step, mine ^ number]
                found.append(pltpu.make_async_copy(source, target, sems.at[which, step, number]))
        return found

    def down_copy(step):
        return pltpu.make_async_copy(down_refs[step].at[0], down_all.at[step], sems.at[2, 0, step])

    for load in loads:
        load.start()
    for step in range(pieces):
        for copy in tile_copies(step):
            copy.start(priority=1)
    for step in range(pieces):
        down_copy(step).start(priority=1)
    for load in loads:
        load.wait()

    squares = jnp.zeros((count, part), F32)
    for number in range(parts):
        held = held_rows[number].astype(F32)
        squares = squares + held * held
    inverse = lax.rsqrt(jnp.sum(squares, axis=1, keepdims=True) / width + 1e-05)
    for number in range(parts):
        lanes = slice(number * part, (number + 1) * part)
        normed[:, lanes] = (held_rows[number].astype(F32) * inverse * gain_ref[:, lanes]).astype(BF16)

    @pl.loop(0, pieces)
    def _(step):
        for copy in tile_copies(step):
            copy.wait()
        held = normed[...]
        gate = jnp.dot(held, gate_all[step].reshape(width, wide), preferred_element_type=F32)
        up = jnp.dot(held, up_all[step].reshape(width, wide), preferred_element_type=F32)
        hidden[step] = (gate / (1.0 + jnp.exp(-gate)) * up).astype(BF16)

    for piece in range(pieces):
        down_copy(piece).wait()

    rows = LANES
    slot_of = lax.broadcasted_iota(jnp.int32, (most, rows), 0).astype(F32) + (expert * most).astype(F32)
    weights, firsts = [], []
    for number in range(some):
        meta = meta_all[number, :, :rows].astype(F32)
        total = jnp.zeros((most, rows), F32)
        for k in range(TOP):
            slot = meta[1 + 2 * k : 2 + 2 * k] * most + meta[2 + 2 * k : 3 + 2 * k]
            line = 1 + 2 * TOP + 3 * k
            weight = meta[line : line + 1] + meta[line + 1 : line + 2] + meta[line + 2 : line + 3]
            total = total + jnp.where(slot_of == slot, weight, 0.0)
            if k == 0:
                firsts.append(jnp.sum(jnp.where(slot_of == slot, 1.0, 0.0), axis=1, keepdims=True))
        weights.append(jnp.sum(total, axis=1, keepdims=True))
    weight = jnp.concatenate(weights, axis=0)
    first = jnp.concatenate(firsts, axis=0)

    stores = []
    for number in range(parts):
        lanes = slice(number * part, (number + 1) * part)
        result = jnp.zeros((count, part), F32)
        for piece in range(pieces):
            result = result + jnp.dot(hidden[piece], down_all[piece, :, lanes], preferred_element_type=F32)
        result = result.astype(BF16).astype(F32) * weight
        result = (held_rows[number].astype(F32) * first + result).astype(BF16)
        for source in range(some):
            answers[source, :, lanes] = result[source * most : (source + 1) * most]
        if number % 2 == 1:
            columns = pl.ds((number - 1) * part, 2 * part)
            for turn in range(some):
                source, target = answers.at[at[turn], :, columns], out_refs[turn].at[:, columns]
                stores.append(pltpu.make_async_copy(source, target, store_sems.at[turn, number // 2]))
                stores[-1].start()
    for store in stores:
        store.wait()


def run_expert(turns, rows, gathered, gain, gates, ups, downs, most):
    blocks = len(rows)
    count, part = len(turns) * most, rows[0].shape[1]
    width = blocks * part
    pieces = len(downs)
    wide = downs[1].shape[1]
    deep = width // pieces
    return pl.pallas_call(
        functools.partial(expert_kernel, pieces, blocks, turns),
        out_shape=[jax.ShapeDtypeStruct((most, width), BF16)] * len(turns),
        in_specs=[pl.BlockSpec(memory_space=pltpu.VMEM)]
        + [ANYWHERE] * (blocks + len(turns) + 3 * pieces),
        out_specs=[ANYWHERE] * len(turns),
        scratch_shapes=[
            pltpu.VMEM((blocks, count, part), BF16),
            pltpu.VMEM((len(turns), META, part), BF16),
            pltpu.VMEM((pieces, pieces, deep, wide), BF16),
            pltpu.VMEM((pieces, pieces, deep, wide), BF16),
            pltpu.VMEM((pieces, wide, width), BF16),
            pltpu.VMEM((count, width), BF16),
            pltpu.VMEM((pieces, count, wide), BF16),
            pltpu.VMEM((len(turns), most, width), BF16),
            pltpu.SemaphoreType.DMA((3, pieces, pieces)),
            pltpu.SemaphoreType.DMA((blocks, 2)),
            pltpu.SemaphoreType.DMA((blocks, blocks // 2)),
        ],
        compiler_params=pltpu.CompilerParams(vmem_limit_bytes=57344 * 1024),
        name="expert_rows",
    )(gain[None, :], *rows, *(gathered[turn] for turn in turns), *gates, *ups, *downs)


def combine_kernel(blocks, slots_ref, *refs):
    row_refs, out_ref = refs[:blocks], refs[blocks]
    most = row_refs[0].shape[0]
    rows = slots_ref.shape[0]
    column = lax.broadcasted_iota(jnp.int32, (rows, blocks * most), 1)
    slot_of = (((column // most) ^ lax.axis_index("expert")) * most + column % most).astype(F32)
    picks = (slot_of == slots_ref[:, 0:1]) | (slot_of == slots_ref[:, 1:2])
    picks = jnp.where(picks, 1.0, 0.0).astype(BF16)
    held = jnp.concatenate([ref[...] for ref in row_refs], axis=0)
    out_ref[0] = jnp.dot(picks, held, preferred_element_type=F32).astype(BF16)


def combine(returned, slots):
    blocks = len(returned)
    width = returned[0].shape[1]
    vmem = pl.BlockSpec(memory_space=pltpu.VMEM)
    return pl.pallas_call(
        functools.partial(combine_kernel, blocks),
        out_shape=jax.ShapeDtypeStruct((1, slots.shape[0], width), BF16),
        in_specs=[vmem] * (1 + blocks),
        out_specs=vmem,
        compiler_params=pltpu.CompilerParams(vmem_limit_bytes=24 * 1024 * 1024),
        name="combine_choices",
    )(slots, *returned)


def flipped(block, axis, bits):
    return lax.ppermute(block, axis, [(i, i ^ bits) for i in range(lax.axis_size(axis))])


def exchange(blocks):
    count = len(blocks)
    moved = {turn: flipped(blocks[turn], "expert", turn) for turn in range(count - 1, 0, -1)}
    return [blocks[0]] + [moved[turn] for turn in range(1, count)]


def per_device(
    queries,
    keys,
    values,
    doc_ids,
    expert_index,
    gates,
    capacity,
    norm_gain,
    gate_weight,
    up_weight,
    down_weight,
):
    rows, width = queries.shape[1:]
    experts = lax.axis_size("expert")
    half = experts // 2
    most = most_of(rows, experts)
    over = lax.axis_size("dp")
    weights = [gate_weight, up_weight, down_weight]
    gate, up, down = ({0: block} for block in weights)
    for number in range(2, over, 2):
        gate[number] = flipped(gate_weight, "dp", number)
    packed, slots = pack(queries, keys, values, doc_ids, expert_index, gates, capacity, experts)
    gathered = exchange(packed)
    gathered, gate, up, down = lax.optimization_barrier((gathered, gate, up, down))
    for pieces in (gate, up, down):
        for number in list(pieces):
            pieces[number + 1] = flipped(pieces[number], "dp", 1)
    for number in range(2, over, 2):
        up[number] = flipped(up_weight, "dp", number)
    routed = list(attend(gathered, most))
    routed, gate, up, down = lax.optimization_barrier((routed, gate, up, down))
    for number in range(2, over, 2):
        down[number] = flipped(down[0], "dp", number)
    received = exchange(routed)
    received, up, down = lax.optimization_barrier((received, up, down))
    for pieces in (up, down):
        for number in range(2, over, 2):
            pieces[number + 1] = flipped(pieces[number], "dp", 1)
    gate, up, down = ([pieces[number] for number in range(over)] for pieces in (gate, up, down))
    received = [block.reshape(experts * most, width // experts) for block in received]
    answered = []
    for turns in (range(half, experts), range(half)):
        answered = [*run_expert(turns, received, gathered, norm_gain, gate, up, down, most), *answered]
    return combine(exchange(answered), slots)


def by_heads(mesh, queries, gate_weight):
    over, experts = mesh.shape["dp"], mesh.shape["expert"]
    rows, width = queries.shape[1] // experts, queries.shape[2]
    hidden = gate_weight.shape[2]
    return (
        width % (experts * HEAD_DIM) == 0
        and rows == LANES
        and WINDOW % rows == 0
        and experts % 4 == 0
        and experts & (experts - 1) == 0
        and width // experts > rows
        and (width // over) % (width // experts) == 0
        and hidden % (over * LANES) == 0
        and most_of(rows, experts) % 16 == 0
        and over > 2
        and over & (over - 1) == 0
        and queries.shape[0] == over
        and gate_weight.shape[0] == experts
    )


def solution(mesh):
    placed = (
        P("dp", "expert", None),
        P("dp", "expert", None),
        P("dp", "expert", None),
        P("dp", "expert"),
        P("dp", "expert", None),
        P("dp", "expert", None),
        P(),
        P(),
        P("expert", "dp", None),
        P("expert", "dp", None),
        P("expert", "dp", None),
    )

    def layer(*arrays):
        step = per_device if by_heads(mesh, arrays[0], arrays[8]) else per_device_general
        return jax.shard_map(
            step, mesh=mesh, in_specs=placed, out_specs=P("dp", "expert", None), check_vma=False
        )(*arrays)

    return layer
```
